32 devices in a mesh: dp: 2 (over y), context: 16 (over z, x, core).
Axes of the slice: x: 2, y: 2, z: 4, core: 2. Of those that a mesh axis runs over, the one named last changes fastest.
Arguments:
- codes: int32 [2, 16384], P('dp', 'context'), may hold values from 0 to 3
- variant_pos: int32 [2, 64], P('dp'), may hold values from 0 to 16383
- variant_shift: int32 [2, 64], P('dp'), may hold values from 1 to 3
- stem_weight: float32 [15, 4, 384], replicated, may hold values from -1.5 to 1.5
- conv_weight: bfloat16 [5, 384, 384], replicated, may hold values from -0.125 to 0.125
- cotangent: bfloat16 [2, 8192, 384], P('dp', 'context'), may hold values from -6 to 6
Outputs:
- features: bfloat16 [2, 8192, 384], P('dp', 'context')
- d_pooled: bfloat16 [2, 8192, 384], P('dp', 'context')
- conv_grad: float32 [5, 384, 384], replicated
- stem_grad: float32 [15, 4, 384], replicated
The draws below stay inside these ranges and needn't reach their ends.
All inputs are finite; a program needn't handle non-finite values.
Results may differ from the reference program's by a relative error of at most 0.009.
Values may be sent and summed in bfloat16 or wider, within the bound.
No kernel may reach another device: no remote copies, remote signals or barrier semaphores. Data moves between devices by JAX's collectives and lax.ppermute only.
A program may use at most 64 MiB of HBM per device.

```python
import math
import jax
import jax.numpy as jnp
from jax import lax

C = 384
VAR = 64
SEQ = 16384
POOLED = 8192
BATCH = 2


def with_ends(array, stream_key, smallest, largest):
    longest = array.shape.index(max(array.shape))
    spots = []
    for shift in (0, 1):
        where = [jax.random.randint(jax.random.fold_in(stream_key, axis), (), 0, length) for axis, length in enumerate(array.shape)]
        where[longest] = (where[longest] + shift) % array.shape[longest]
        spots.append(tuple(where))
    return array.at[spots[0]].set(smallest).at[spots[1]].set(largest)


def level_of(key, shape, shards, smallest, high):
    gain = 1.0
    for position, blocks in shards:
        draws = jax.random.uniform(jax.random.fold_in(jax.random.fold_in(key, 6), position), (blocks,), jnp.float32, smallest / len(shards), high / len(shards))
        gain = gain * jnp.repeat(jnp.exp(draws), shape[position] // blocks).reshape((-1,) + (1,) * (len(shape) - 1 - position))
    return gain


def scatter_about(key, dims, spread, most, split=(), kind=jnp.bfloat16):
    result = jax.random.normal(key, dims, jnp.float32) * spread
    if len(split) > 0:
        result = level_of(key, dims, split, -0.22, 0.18) * result
    return jnp.clip(result, min=-most, max=most).astype(kind)


def setup_inputs(seed: int = 0) -> dict:
    arg_keys = jax.random.split(jax.random.key(seed), 7)
    codes = with_ends(jax.random.randint(arg_keys[0], (BATCH, SEQ), 0, 4), jax.random.fold_in(arg_keys[0], 1), 0, 3).astype(jnp.int32)
    variant_pos = with_ends(jax.random.randint(arg_keys[1], (BATCH, VAR), 0, SEQ), jax.random.fold_in(arg_keys[1], 1), 0, SEQ - 1).astype(jnp.int32)
    variant_shift = with_ends(jax.random.randint(arg_keys[2], (BATCH, VAR), 1, 4), jax.random.fold_in(arg_keys[2], 1), 1, 3).astype(jnp.int32)
    stem_weight = scatter_about(arg_keys[3], (15, 4, C), 15 ** -0.5, 1.5, (), jnp.float32)
    conv_weight = scatter_about(arg_keys[4], (5, C, C), (5 * C) ** -0.5, 0.125)
    cotangent = scatter_about(arg_keys[5], (BATCH, POOLED, C), 1.0, 6.0, ((0, 2), (1, 16)))
    return dict(codes=codes, variant_pos=variant_pos, variant_shift=variant_shift, stem_weight=stem_weight, conv_weight=conv_weight, cotangent=cotangent)


root_scale = math.sqrt(2.0 / math.pi)
cubic = 0.044715

def gelu_tanh(value):
    return 0.5 * value * (1.0 + jnp.tanh(root_scale * (value + cubic * value * value * value)))

def gelu_slope(value):
    inner = jnp.tanh(root_scale * (value + cubic * value * value * value))
    return 0.5 * (1.0 + inner) + 0.5 * value * (1.0 - inner * inner) * root_scale * (1.0 + 3.0 * cubic * value * value)

def reference(codes, variant_pos, variant_shift, stem_weight, conv_weight, cotangent):
    length = codes.shape[1]
    rows = length // 2
    width = stem_weight.shape[2]
    flat_stem = stem_weight.reshape(60, width)

    def one_sequence(carry, items):
        conv_total, stem_total = carry
        base_row, positions, amounts, cot_row = items
        shifts = jnp.zeros((length,), jnp.int32).at[positions].add(amounts)
        mutated = (base_row + shifts) % 4
        onehot = (mutated[:, None] == jnp.arange(4, dtype=jnp.int32)[None, :]).astype(jnp.float32)
        padded = jnp.pad(onehot, ((7, 7), (0, 0)))
        windows = jnp.concatenate([padded[k:k + length] for k in range(15)], axis=1)
        stem = jnp.dot(windows, flat_stem, precision=lax.Precision.HIGHEST, preferred_element_type=jnp.float32)
        active = gelu_tanh(stem)
        pooled = (0.5 * (active[0::2] + active[1::2])).astype(jnp.bfloat16)
        pooled_f = pooled.astype(jnp.float32)
        gated = gelu_tanh(pooled_f).astype(jnp.bfloat16)
        gated_pad = jnp.pad(gated, ((2, 2), (0, 0)))
        conv_out = jnp.zeros((rows, width), jnp.float32)
        for offset in range(5):
            conv_out = conv_out + jnp.dot(gated_pad[offset:offset + rows], conv_weight[offset], preferred_element_type=jnp.float32)
        features = (pooled_f + conv_out).astype(jnp.bfloat16)
        cot_pad = jnp.pad(cot_row, ((2, 2), (0, 0)))
        back = jnp.zeros((rows, width), jnp.float32)
        for offset in range(5):
            back = back + jnp.dot(cot_pad[4 - offset:4 - offset + rows], conv_weight[offset].T, preferred_element_type=jnp.float32)
        dpool = cot_row.astype(jnp.float32) + back * gelu_slope(pooled_f)
        grads = jnp.stack([jnp.dot(gated_pad[offset:offset + rows].T, cot_row, preferred_element_type=jnp.float32) for offset in range(5)])
        dstem = 0.5 * jnp.repeat(dpool, 2, axis=0) * gelu_slope(stem)
        stem_part = jnp.dot(windows.T, dstem, precision=lax.Precision.HIGHEST, preferred_element_type=jnp.float32)
        return ((conv_total + grads, stem_total + stem_part), (features, dpool.astype(jnp.bfloat16)))
    init = (jnp.zeros((5, width, width), jnp.float32), jnp.zeros((60, width), jnp.float32))
    (conv_grad, stem_grad), (features, d_pooled) = lax.scan(one_sequence, init, (codes, variant_pos, variant_shift, cotangent))
    return (features, d_pooled, conv_grad, stem_grad.reshape(15, 4, width))
```

```python
import functools
import math

import jax
import jax.numpy as jnp
from jax import lax
from jax.experimental import pallas as pl
from jax.experimental.pallas import tpu as pltpu
from jax.sharding import PartitionSpec as P

root_scale = math.sqrt(2.0 / math.pi)
cubic = 0.044715
AXES = ("dp", "context")
TAPS = 5
HALO = 6
LEAD = 16
VMEM = pl.BlockSpec(memory_space=pltpu.VMEM)
SMEM = pl.BlockSpec(memory_space=pltpu.SMEM)
bf16 = jnp.bfloat16
f32 = jnp.float32


def gelu_tanh(value):
    inner = jnp.tanh(value * (root_scale + (root_scale * cubic) * (value * value)))
    half = 0.5 * value
    return half + half * inner


def gelu_slope(value):
    square = value * value
    inner = jnp.tanh(value * (root_scale + (root_scale * cubic) * square))
    rise = (1.0 - inner * inner) * (root_scale + (3.0 * root_scale * cubic) * square)
    return 0.5 + 0.5 * inner + (0.5 * value) * rise


def rounded(value):
    return lax.reduce_precision(value, 8, 7)


def params(limit=48):
    return pltpu.CompilerParams(vmem_limit_bytes=limit * 1024 * 1024)


def first_kernel(rows, lanes, codes, place, positions, amounts, top, bottom, own, near, far):
    length = 2 * rows
    tiles = length // 128
    base = place[0]
    core = place[1]
    x = jnp.concatenate([codes[:, 128 * q : 128 * q + 128] for q in range(tiles)], axis=0)
    spot = (
        base
        + 128 * lax.broadcasted_iota(jnp.int32, x.shape, 0)
        + lax.broadcasted_iota(jnp.int32, x.shape, 1)
    )
    for v in range(positions.shape[1]):
        x = x + jnp.where(spot == positions[0, v], amounts[0, v], 0)
    x = ((x & 3) + 1).astype(f32).astype(bf16)
    source = lax.broadcasted_iota(jnp.int32, (128, 128), 0)
    target = lax.broadcasted_iota(jnp.int32, (128, 128), 1)

    def picked(parity):
        left = (source == 2 * target + parity).astype(f32).astype(bf16)
        right = (source == 2 * (target - 64) + parity).astype(f32).astype(bf16)
        low = jnp.dot(x, left, preferred_element_type=f32)
        high = jnp.dot(x, right, preferred_element_type=f32)
        parts = [low[2 * q : 2 * q + 1] + high[2 * q + 1 : 2 * q + 2] for q in range(tiles // 2)]
        return jnp.concatenate(parts + [jnp.zeros((1, lanes - rows), f32)], axis=1)

    both = jnp.concatenate([picked(0), picked(1), jnp.zeros((6, lanes), f32)], axis=0)
    lane = lax.broadcasted_iota(jnp.int32, both.shape, 1)
    shifted = pltpu.roll(both, HALO, 1)
    last = jnp.where(lane < HALO, pltpu.roll(both, lanes - (rows - HALO), 1), 0.0)
    ahead = (lane >= rows + HALO) & (lane < rows + 2 * HALO)
    first = jnp.where(ahead, pltpu.roll(both, rows + HALO, 1), 0.0)
    blank = jnp.zeros((8, lanes), f32)
    width = top.shape[1]
    pad = jnp.zeros((2, lanes - width), f32)
    rest = jnp.zeros((4, lanes), f32)

    def message(edge, cot):
        cot = jnp.concatenate([cot, pad], axis=1)
        return jnp.concatenate([edge, cot, jnp.zeros((6, lanes), f32)], axis=0)

    first_rows = top[...].astype(f32)[0:2]
    last_rows = bottom[...].astype(f32)[14:16]
    del rest
    head = message(first, first_rows)
    tail = message(last, last_rows)
    own[...] = jnp.concatenate([shifted, blank], axis=0).astype(bf16)
    near[...] = jnp.where(core == 0, tail, head).astype(bf16)
    far[...] = jnp.where(core == 0, head, tail).astype(bf16)


def weight_kernel(weight, out):
    width = weight.shape[2]
    zero = jnp.zeros((1, width), f32)
    taps = weight.shape[0]

    def rows(order):
        return jnp.concatenate(
            [
                zero if k is None else weight[k, a : a + 1, :]
                for a in range(4)
                for k in order
            ],
            axis=0,
        )

    even = [None] + list(range(taps - 2, 0, -2)) + list(range(taps - 1, -1, -2))
    odd = list(range(taps - 1, -1, -2)) + list(range(taps - 2, 0, -2)) + [None]
    full = jnp.concatenate([rows(even), rows(odd)], axis=1)
    high = full.astype(bf16)
    left = full - high.astype(f32)
    middle = left.astype(bf16)
    low = (left - middle.astype(f32)).astype(bf16)
    out[...] = jnp.concatenate([high, middle, low], axis=0)


def one_hot(codes, lanes, shift):
    even = jnp.broadcast_to(codes[0:1], (8, lanes))
    odd = jnp.broadcast_to(codes[1:2], (8, lanes))
    even = pltpu.roll(even, (2 * lanes - 8 + shift) % lanes, 1, stride=1, stride_axis=0)
    odd = pltpu.roll(odd, (2 * lanes - 7 + shift) % lanes, 1, stride=1, stride_axis=0)
    near = jnp.concatenate([even, odd], axis=0)
    return jnp.concatenate([(near == a + 1.0).astype(f32) for a in range(4)], axis=0).astype(bf16)


def conv_kernel(rows, total, place, own, near, far, weight, cot, out, stem, gated):
    lanes = own.shape[1]
    used = rows + 128
    width = cot.shape[1]
    codes = (own[...].astype(f32) + near[...].astype(f32) + far[...].astype(f32))[0:8]
    hot = one_hot(codes, lanes, 0)[:, :used]
    hot = jnp.concatenate([hot, hot, hot], axis=0)
    stem[...] = lax.dot_general(
        weight[...], hot, (((0,), (0,)), ((), ())), preferred_element_type=f32
    )
    spot = place[2] - 2 + lax.broadcasted_iota(jnp.int32, (1, used), 1)
    inside = (spot >= 0) & (spot < total)
    step = 16
    for c in range(0, width, step):
        even = gelu_tanh(stem[c : c + step, :])
        odd = gelu_tanh(stem[width + c : width + c + step, :])
        pooled = (0.5 * (even + odd)).astype(bf16).astype(f32)
        value = jnp.where(inside, gelu_tanh(pooled), 0.0)
        for t in range(TAPS):
            moved = value if t == 0 else pltpu.roll(value, used - t, 1)
            gated[t * width + c : t * width + c + step, :] = moved[:, :rows].astype(bf16)
    out[...] = jnp.dot(gated[...], cot[...], preferred_element_type=f32).astype(bf16)


def back_kernel(
    rows, total, place, own, near, far, weight, conv, cot, d_pooled, stem_part, gated, pooled, stem, ext
):
    lanes = own.shape[1]
    width = cot.shape[1]
    padded = rows + 2 * LEAD
    core = place[1]
    near_v = near[...].astype(f32)
    far_v = far[...].astype(f32)
    codes = (own[...].astype(f32) + near_v + far_v)[0:8]
    hot = one_hot(codes, lanes, LEAD - 2)[:, :padded]
    hot = jnp.concatenate([hot, hot, hot], axis=0)
    stem[...] = lax.dot_general(
        hot, weight[...], (((0,), (0,)), ((), ())), preferred_element_type=f32
    )
    before = jnp.where(core == 0, far_v, near_v)[8:10, :width]
    after = jnp.where(core == 0, near_v, far_v)[8:10, :width]
    gap = jnp.zeros((LEAD - 2, width), f32)
    ext[0:LEAD, :] = jnp.concatenate([gap, before], axis=0).astype(bf16)
    ext[LEAD : LEAD + rows, :] = cot[...]
    ext[LEAD + rows :, :] = jnp.concatenate([after, gap], axis=0).astype(bf16)
    step = 128
    mine = one_hot(codes, lanes, lanes - 2)
    acc = jnp.zeros((64, 2 * width), f32)
    for edge in (0, LEAD + rows):
        act = 0.5 * (
            gelu_tanh(stem[edge : edge + LEAD, :width]) + gelu_tanh(stem[edge : edge + LEAD, width:])
        )
        act = act.astype(bf16).astype(f32)
        spot = place[2] - LEAD + edge + lax.broadcasted_iota(jnp.int32, (LEAD, 1), 0)
        inside = (spot >= 0) & (spot < total)
        gated[edge : edge + LEAD, :] = jnp.where(inside, gelu_tanh(act), 0.0).astype(bf16)
    for r in range(0, rows, step):
        back = jnp.zeros((step, width), f32)
        for t in range(TAPS):
            start = LEAD + 2 - t + r
            back = back + lax.dot_general(
                ext[start : start + step, :],
                conv[t],
                (((1,), (1,)), ((), ())),
                preferred_element_type=f32,
            )
        even = stem[LEAD + r : LEAD + r + step, :width]
        odd = stem[LEAD + r : LEAD + r + step, width:]
        low = (0.5 * (gelu_tanh(even) + gelu_tanh(odd))).astype(bf16)
        value = low.astype(f32)
        pooled[r : r + step, :] = low
        gated[LEAD + r : LEAD + r + step, :] = gelu_tanh(value).astype(bf16)
        grad = cot[r : r + step, :].astype(f32) + back * gelu_slope(value)
        d_pooled[r : r + step, :] = grad.astype(bf16)
        half = 0.5 * grad
        terms = jnp.concatenate([half * gelu_slope(even), half * gelu_slope(odd)], axis=1)
        acc = acc + jnp.dot(mine[:, r : r + step], terms.astype(bf16), preferred_element_type=f32)
    stem_part[...] = acc


def feature_kernel(rows, gated, pooled, conv, out):
    step = 128
    for r in range(0, rows, step):
        acc = pooled[r : r + step, :].astype(f32)
        for t in range(TAPS):
            start = LEAD - 2 + t + r
            acc = acc + jnp.dot(gated[start : start + step, :], conv[t], preferred_element_type=f32)
        out[r : r + step, :] = acc.astype(bf16)


def stem_rows(part, taps, width):
    grid = part.reshape(4, 16, 2 * width)
    even, odd = grid[:, :, :width], grid[:, :, width:]
    place_even = [None] + list(range(taps - 2, 0, -2)) + list(range(taps - 1, -1, -2))
    place_odd = list(range(taps - 1, -1, -2)) + list(range(taps - 2, 0, -2)) + [None]
    return jnp.stack(
        [even[:, place_even.index(k)] + odd[:, place_odd.index(k)] for k in range(taps)], axis=0
    )


def per_device(codes, variant_pos, variant_shift, stem_weight, conv_weight, cotangent):
    n_dp, n_ctx = lax.axis_size("dp"), lax.axis_size("context")
    devices = n_dp * n_ctx
    length = codes.shape[1]
    rows = length // 2
    taps, _, width = stem_weight.shape
    total = rows * n_ctx
    lanes = -(-(rows + 256) // 128) * 128
    ctx = lax.axis_index("context")
    rank = lax.axis_index("dp") * n_ctx + ctx
    core = ctx % 2
    place = jnp.stack([ctx * length, core, ctx * rows]).astype(jnp.int32)
    cot = cotangent[0]

    own, near, far = pl.pallas_call(
        functools.partial(first_kernel, rows, lanes),
        grid=(1,),
        out_shape=[jax.ShapeDtypeStruct((16, lanes), bf16)] * 3,
        in_specs=[
            pl.BlockSpec((1, length), lambda i: (0, 0)),
            SMEM,
            SMEM,
            SMEM,
            pl.BlockSpec((16, width), lambda i: (0, 0)),
            pl.BlockSpec((16, width), lambda i: (rows // 16 - 1, 0)),
        ],
        out_specs=[pl.BlockSpec((16, lanes), lambda i: (0, 0))] * 3,
        compiler_params=params(),
    )(codes, place, variant_pos, variant_shift, cot, cot)

    def swap(value, even_bit, odd_bit):
        pairs = [(i, i ^ (odd_bit if i & 1 else even_bit)) for i in range(devices)]
        return lax.ppermute(value, AXES, pairs)

    def bit(even_bit, odd_bit):
        return (rank // jnp.where(core == 1, odd_bit, even_bit)) % 2

    outward = []
    for d in range(n_dp):
        for c in range(n_ctx):
            other = c + 1 if c & 1 else c - 1
            if 0 <= other < n_ctx:
                outward.append((d * n_ctx + c, d * n_ctx + other))
    near = swap(near, 1, 1)
    far = lax.ppermute(far, AXES, outward)

    weight = pl.pallas_call(
        weight_kernel,
        out_shape=jax.ShapeDtypeStruct((192, 2 * width), bf16),
        in_specs=[VMEM],
        out_specs=VMEM,
        compiler_params=params(),
    )(stem_weight)

    part = pl.pallas_call(
        functools.partial(conv_kernel, rows, total),
        out_shape=jax.ShapeDtypeStruct((TAPS * width, width), bf16),
        in_specs=[SMEM] + [VMEM] * 5,
        out_specs=VMEM,
        scratch_shapes=[
            pltpu.VMEM((2 * width, rows + 128), f32),
            pltpu.VMEM((TAPS * width, rows), bf16),
        ],
        compiler_params=params(),
    )(place, own, near, far, weight, cot)

    padded = rows + 2 * LEAD
    d_pooled, stem_part, gated, pooled = pl.pallas_call(
        functools.partial(back_kernel, rows, total),
        out_shape=[
            jax.ShapeDtypeStruct((rows, width), bf16),
            jax.ShapeDtypeStruct((64, 2 * width), f32),
            jax.ShapeDtypeStruct((padded, width), bf16),
            jax.ShapeDtypeStruct((rows, width), bf16),
        ],
        in_specs=[SMEM] + [VMEM] * 6,
        out_specs=[VMEM] * 4,
        scratch_shapes=[
            pltpu.VMEM((padded, 2 * width), f32),
            pltpu.VMEM((padded, width), bf16),
        ],
        compiler_params=params(),
        cost_estimate=pl.CostEstimate(
            flops=2 * TAPS * rows * width * width, bytes_accessed=4 << 20, transcendentals=0
        ),
    )(place, own, near, far, weight, conv_weight, cot)

    features = pl.pallas_call(
        functools.partial(feature_kernel, rows),
        out_shape=jax.ShapeDtypeStruct((rows, width), bf16),
        in_specs=[VMEM] * 3,
        out_specs=VMEM,
        compiler_params=params(),
        cost_estimate=pl.CostEstimate(
            flops=2 * TAPS * rows * width * width, bytes_accessed=4 << 20, transcendentals=0
        ),
    )(gated, pooled, conv_weight)

    x_bit, y_bit = 2, n_ctx
    split = [(1, 1), (x_bit, y_bit), (y_bit, x_bit)]
    others = [1 << k for k in range(devices.bit_length() - 1) if (1 << k) not in (1, x_bit, y_bit)]
    value = part.astype(f32)
    size = value.shape[0]
    for pair in split:
        size //= 2
        which = bit(*pair)
        low = value.astype(bf16)
        sent = lax.dynamic_slice_in_dim(low, (1 - which) * size, size, 0)
        kept = lax.dynamic_slice_in_dim(low, which * size, size, 0)
        value = kept.astype(f32) + swap(sent, *pair).astype(f32)
    stem_sum = stem_rows(stem_part, taps, width).reshape(4 * taps, width)
    for b in others:
        both = rounded(jnp.concatenate([value, stem_sum], axis=0))
        both = both + swap(both.astype(bf16), b, b).astype(f32)
        value, stem_sum = both[:size], both[size:]
    value = value.astype(bf16)
    for pair in split[::-1]:
        stem_sum = rounded(stem_sum)
        got = swap(jnp.concatenate([value, stem_sum.astype(bf16)], axis=0), *pair)
        stem_sum = stem_sum + got[size:].astype(f32)
        got = got[:size]
        which = bit(*pair)
        value = jnp.where(
            which == 0, jnp.concatenate([value, got], axis=0), jnp.concatenate([got, value], axis=0)
        )
        size *= 2
    conv_grad = value.astype(f32).reshape(TAPS, width, width)
    stem_grad = stem_sum.reshape(taps, 4, width)
    return (features[None], d_pooled[None], conv_grad, stem_grad)


def solution(mesh):
    placed = (P("dp", "context"), P("dp", None), P("dp", None), P(), P(), P("dp", "context", None))
    return jax.shard_map(
        per_device,
        mesh=mesh,
        in_specs=placed,
        out_specs=(P("dp", "context", None), P("dp", "context", None), P(), P()),
        check_vma=False,
    )
```

```python
import functools
import math

import jax
import jax.numpy as jnp
from jax import lax
from jax.experimental import pallas as pl
from jax.experimental.pallas import tpu as pltpu
from jax.sharding import PartitionSpec as P

root_scale = math.sqrt(2.0 / math.pi)
cubic = 0.044715
AXES = ("dp", "context")
TAPS = 5
HALO = 6
LEAD = 16
VMEM = pl.BlockSpec(memory_space=pltpu.VMEM)
FAR = pl.BlockSpec(memory_space=pltpu.HBM)
bf16 = jnp.bfloat16
f32 = jnp.float32


def gelu_tanh(value):
    inner = jnp.tanh(value * (root_scale + (root_scale * cubic) * (value * value)))
    half = 0.5 * value
    return half + half * inner


def gelu_both(value):
    square = value * value
    inner = jnp.tanh(value * (root_scale + (root_scale * cubic) * square))
    rise = (1.0 - inner * inner) * (root_scale + (3.0 * root_scale * cubic) * square)
    half = 0.5 * value
    return half + half * inner, 0.5 + 0.5 * inner + half * rise


def rounded(value):
    return lax.reduce_precision(value, 8, 7)


def params(limit=24):
    return pltpu.CompilerParams(vmem_limit_bytes=limit * 1024 * 1024)


def after(value, *others):
    return lax.optimization_barrier((value,) + others)[0]


def first_kernel(
    rows, lanes, codes, positions, amounts, cot, own, near, far, msg, base_v, pos_s, amt_s, top, bottom, sems
):
    length = 2 * rows
    tiles = length // 128
    width = cot.shape[1]
    copies = [
        pltpu.make_async_copy(codes, base_v, sems.at[0]),
        pltpu.make_async_copy(positions, pos_s, sems.at[1]),
        pltpu.make_async_copy(amounts, amt_s, sems.at[2]),
        pltpu.make_async_copy(cot.at[pl.ds(0, 16)], top, sems.at[3]),
        pltpu.make_async_copy(cot.at[pl.ds(rows - 16, 16)], bottom, sems.at[4]),
        pltpu.make_async_copy(cot, msg.at[pl.ds(0, rows)], sems.at[5]),
    ]
    for copy in copies:
        copy.start()
    ctx = lax.axis_index("context")
    core = lax.rem(ctx, 2)
    for copy in copies[:5]:
        copy.wait()
    x = jnp.concatenate([base_v[:, 128 * q : 128 * q + 128] for q in range(tiles)], axis=0)
    spot = (
        ctx * length
        + 128 * lax.broadcasted_iota(jnp.int32, x.shape, 0)
        + lax.broadcasted_iota(jnp.int32, x.shape, 1)
    )
    sums = [x] + [jnp.zeros_like(x)] * 3
    for v in range(positions.shape[1]):
        sums[v % 4] = sums[v % 4] + jnp.where(spot == pos_s[0, v], amt_s[0, v], 0)
    x = (sums[0] + sums[1]) + (sums[2] + sums[3])
    x = ((x & 3) + 1).astype(f32).astype(bf16)
    source = lax.broadcasted_iota(jnp.int32, (128, 128), 0)
    target = lax.broadcasted_iota(jnp.int32, (128, 128), 1)

    def picked(parity):
        left = (source == 2 * target + parity).astype(f32).astype(bf16)
        right = (source == 2 * (target - 64) + parity).astype(f32).astype(bf16)
        low = jnp.dot(x, left, preferred_element_type=f32)
        high = jnp.dot(x, right, preferred_element_type=f32)
        parts = [low[2 * q : 2 * q + 1] + high[2 * q + 1 : 2 * q + 2] for q in range(tiles // 2)]
        return jnp.concatenate(parts + [jnp.zeros((1, lanes - rows), f32)], axis=1)

    both = jnp.concatenate([picked(0), picked(1), jnp.zeros((6, lanes), f32)], axis=0)
    lane = lax.broadcasted_iota(jnp.int32, both.shape, 1)
    shifted = pltpu.roll(both, HALO, 1)
    last = jnp.where(lane < HALO, pltpu.roll(both, lanes - (rows - HALO), 1), 0.0)
    ahead = (lane >= rows + HALO) & (lane < rows + 2 * HALO)
    first = jnp.where(ahead, pltpu.roll(both, rows + HALO, 1), 0.0)
    blank = jnp.zeros((8, lanes), f32)
    pad = jnp.zeros((2, lanes - width), f32)

    def message(edge, grads):
        grads = jnp.concatenate([grads, pad], axis=1)
        return jnp.concatenate([edge, grads, jnp.zeros((6, lanes), f32)], axis=0)

    head = message(first, top[...].astype(f32)[0:2])
    tail = message(last, bottom[...].astype(f32)[14:16])
    own[...] = jnp.concatenate([shifted, blank], axis=0).astype(bf16)
    near[...] = jnp.where(core == 0, tail, head).astype(bf16)
    far[...] = jnp.where(core == 0, head, tail).astype(bf16)
    copies[5].wait()


def message_kernel(own, near, whole, msg):
    del whole
    width = msg.shape[1]
    codes = (own[...].astype(f32) + near[...].astype(f32))[0:2]
    blank = jnp.zeros((1, 2 * width - codes.shape[1]), f32)
    lines = []
    for k in range(2):
        line = codes[k : k + 1]
        if blank.shape[1]:
            line = jnp.concatenate([line, blank], axis=1)
        lines += [line[:, :width], line[:, width:]]
    lines.append(jnp.zeros((12, width), f32))
    msg[...] = jnp.concatenate(lines, axis=0).astype(bf16)


def weight_kernel(weight, out, half_out):
    width = weight.shape[2]
    zero = jnp.zeros((1, width), f32)
    even, odd = orders(weight.shape[0])

    def rows(order):
        return jnp.concatenate(
            [
                zero if k is None else weight[k, a : a + 1, :]
                for a in range(4)
                for k in order
            ],
            axis=0,
        )

    def terms(full):
        high = full.astype(bf16)
        left = full - high.astype(f32)
        middle = left.astype(bf16)
        low = (left - middle.astype(f32)).astype(bf16)
        return jnp.concatenate([high, middle, low], axis=0)

    evens, odds = rows(even), rows(odd)
    half = width // 2
    upper = lax.rem(lax.axis_index("dp"), 2) == 1
    out[...] = terms(jnp.concatenate([evens, odds], axis=1))
    mine = [jnp.where(upper, v[:, half:], v[:, :half]) for v in (evens, odds)]
    half_out[...] = terms(jnp.concatenate(mine, axis=1))


def orders(taps):
    even = [None] + list(range(taps - 2, 0, -2)) + list(range(taps - 1, -1, -2))
    odd = list(range(taps - 1, -1, -2)) + list(range(taps - 2, 0, -2)) + [None]
    return even, odd


def one_hot(codes, lanes, shift):
    even = jnp.broadcast_to(codes[0:1], (8, lanes))
    odd = jnp.broadcast_to(codes[1:2], (8, lanes))
    even = pltpu.roll(even, (2 * lanes - 8 + shift) % lanes, 1, stride=1, stride_axis=0)
    odd = pltpu.roll(odd, (2 * lanes - 7 + shift) % lanes, 1, stride=1, stride_axis=0)
    near = jnp.concatenate([even, odd], axis=0)
    return jnp.concatenate([(near == a + 1.0).astype(f32) for a in range(4)], axis=0).astype(bf16)


def shifted_gates(codes, first, total, weight, rows, stem, gated):
    used = rows + 128
    half = weight.shape[1] // 2
    hot = one_hot(codes, codes.shape[1], 0)[:, :used]
    hot = jnp.concatenate([hot, hot, hot], axis=0)
    stem[...] = lax.dot_general(
        weight[...], hot, (((0,), (0,)), ((), ())), preferred_element_type=f32
    )
    spot = first - 2 + lax.broadcasted_iota(jnp.int32, (1, used), 1)
    inside = (spot >= 0) & (spot < total)
    step = 16
    for c in range(0, half, step):
        even = gelu_tanh(stem[c : c + step, :])
        odd = gelu_tanh(stem[half + c : half + c + step, :])
        pooled = (0.5 * (even + odd)).astype(bf16).astype(f32)
        value = jnp.where(inside, gelu_tanh(pooled), 0.0)
        for t in range(TAPS):
            moved = value if t == 0 else pltpu.roll(value, used - t, 1)
            gated[t * half + c : t * half + c + step, :] = moved[:, :rows].astype(bf16)


def own_kernel(rows, total, own, near, far, weight, cot, out, stem, gated, cot_v, sem):
    copy = pltpu.make_async_copy(cot, cot_v, sem)
    copy.start()
    first = lax.axis_index("context") * rows
    codes = (own[...].astype(f32) + near[...].astype(f32) + far[...].astype(f32))[0:8]
    shifted_gates(codes, first, total, weight, rows, stem, gated)
    copy.wait()
    out[...] = jnp.dot(gated[...], cot_v[...], preferred_element_type=f32)


def pair_kernel(rows, total, part, msg, far, weight, sent, kept, stem, gated):
    lanes = far.shape[1]
    ctx = lax.axis_index("context")
    core = lax.rem(ctx, 2)
    extra = msg[rows : rows + 16, :].astype(f32)
    lines = [jnp.concatenate([extra[2 * k : 2 * k + 1], extra[2 * k + 1 : 2 * k + 2]], axis=1) for k in range(2)]
    lines = [line[:, :lanes] for line in lines]
    codes = jnp.concatenate(lines + [jnp.zeros((6, lanes), f32)], axis=0) + far[...].astype(f32)[0:8]
    shifted_gates(codes, ctx * rows, total, weight, rows, stem, gated)
    size = sent.shape[0]
    for which, out in ((1 - core, sent), (core, kept)):
        span = pl.ds(pl.multiple_of(which * size, 16), size)
        value = part[span, :] + jnp.dot(
            gated[span, :], msg[0:rows, :], preferred_element_type=f32
        )
        out[...] = value.astype(out.dtype)


def back_kernel(
    rows, total, own, near, far, weight, conv, cot, d_pooled, stem_part, gated, pooled, stem, ext, back, conv_v, cot_v, sems
):
    copies = [
        pltpu.make_async_copy(cot, cot_v, sems.at[0]),
        pltpu.make_async_copy(conv, conv_v, sems.at[1]),
    ]
    for copy in copies:
        copy.start()
    lanes = own.shape[1]
    width = cot.shape[1]
    padded = rows + 2 * LEAD
    ctx = lax.axis_index("context")
    core = lax.rem(ctx, 2)
    near_v = near[...].astype(f32)
    far_v = far[...].astype(f32)
    codes = (own[...].astype(f32) + near_v + far_v)[0:8]
    hot = one_hot(codes, lanes, LEAD - 2)[:, :padded]
    hot = jnp.concatenate([hot, hot, hot], axis=0)
    stem[...] = lax.dot_general(
        hot, weight[...], (((0,), (0,)), ((), ())), preferred_element_type=f32
    )
    before = jnp.where(core == 0, far_v, near_v)[8:10, :width]
    behind = jnp.where(core == 0, near_v, far_v)[8:10, :width]
    gap = jnp.zeros((LEAD - 2, width), f32)
    ext[0:LEAD, :] = jnp.concatenate([gap, before], axis=0).astype(bf16)
    ext[LEAD + rows :, :] = jnp.concatenate([behind, gap], axis=0).astype(bf16)
    mine = one_hot(codes, lanes, lanes - 2)
    for edge in (0, LEAD + rows):
        act = 0.5 * (
            gelu_tanh(stem[edge : edge + LEAD, :width]) + gelu_tanh(stem[edge : edge + LEAD, width:])
        )
        act = act.astype(bf16).astype(f32)
        spot = ctx * rows - LEAD + edge + lax.broadcasted_iota(jnp.int32, (LEAD, 1), 0)
        inside = (spot >= 0) & (spot < total)
        gated[edge : edge + LEAD, :] = jnp.where(inside, gelu_tanh(act), 0.0).astype(bf16)
    for copy in copies:
        copy.wait()
    ext[LEAD : LEAD + rows, :] = cot_v[...]
    for t in range(TAPS):
        start = LEAD + 2 - t
        term = lax.dot_general(
            ext[start : start + rows, :], conv_v[t], (((1,), (1,)), ((), ())), preferred_element_type=f32
        )
        back[...] = term if t == 0 else back[...] + term
    step = 32
    for r in range(0, rows, step):
        even = stem[LEAD + r : LEAD + r + step, :width]
        odd = stem[LEAD + r : LEAD + r + step, width:]
        even, even_slope = gelu_both(even)
        odd, odd_slope = gelu_both(odd)
        low = (0.5 * (even + odd)).astype(bf16)
        pooled[r : r + step, :] = low
        gate, slope = gelu_both(low.astype(f32))
        gated[LEAD + r : LEAD + r + step, :] = gate.astype(bf16)
        grad = cot_v[r : r + step, :].astype(f32) + back[r : r + step, :] * slope
        d_pooled[r : r + step, :] = grad.astype(bf16)
        half = 0.5 * grad
        stem[LEAD + r : LEAD + r + step, :width] = half * even_slope
        stem[LEAD + r : LEAD + r + step, width:] = half * odd_slope
    grads = jnp.dot(
        mine[:, :rows], stem[LEAD : LEAD + rows, :].astype(bf16), preferred_element_type=f32
    )
    even, odd = orders(stem_part.shape[0] // 4 - 1)
    for k in range(len(even) - 1):
        for a in range(4):
            p, q = 16 * a + even.index(k), 16 * a + odd.index(k)
            stem_part[4 * k + a : 4 * k + a + 1, :] = (
                grads[p : p + 1, :width] + grads[q : q + 1, width:]
            )
    stem_part[stem_part.shape[0] - 4 :, :] = jnp.zeros((4, width), f32)


def feature_kernel(rows, gated, pooled, conv, out, conv_v, sem):
    copy = pltpu.make_async_copy(conv, conv_v, sem)
    copy.start()
    copy.wait()
    acc = pooled[...].astype(f32)
    for t in range(TAPS):
        start = LEAD - 2 + t
        acc = acc + jnp.dot(gated[start : start + rows, :], conv_v[t], preferred_element_type=f32)
    out[...] = acc.astype(bf16)


def place_units(pieces, sizes, offsets, unit, size, bits, out, room, sems):
    copies = []
    for piece, count, offset in zip(pieces, sizes, offsets):
        for p, (x, y, core) in enumerate(bits):
            for u in range(count // unit):
                n = len(copies)
                at = (2 * core + x) * (size // unit) + offset // unit + u
                per_tap = out.shape[0] // (2 * TAPS * unit)
                tap = at // per_tap
                row = (2 * tap + y) * (per_tap * unit) + (at - tap * per_tap) * unit
                room[n * unit : (n + 1) * unit, :] = piece[
                    p * count + u * unit : p * count + (u + 1) * unit, :
                ].astype(f32)
                copy = pltpu.make_async_copy(
                    room.at[pl.ds(n * unit, unit)],
                    out.at[pl.ds(pl.multiple_of(row, 8), unit)],
                    sems.at[n],
                )
                copy.start()
                copies.append(copy)
    for copy in copies:
        copy.wait()


def piece_bits(flip, order_first, order_second):
    ctx = lax.axis_index("context")
    core = lax.rem(ctx, 2)
    x = lax.rem(ctx // 2, 2)
    y = lax.rem(lax.axis_index("dp"), 2)
    x_first = jnp.where(core == 0, order_first, order_second)
    x_first = jnp.where(flip == 1, 1 - x_first, x_first)
    result = []
    for p in range(4):
        one, two = p % 2, p // 2
        dx = jnp.where(x_first == 1, one, two)
        dy = one + two - dx
        result.append((lax.rem(x + dx, 2), lax.rem(y + dy, 2), lax.rem(core + flip, 2)))
    return result


def place_kernel(flip, sizes, offsets, unit, size, left, right, *rest):
    if flip:
        stem, whole, out, stem_out, room, sems = rest
        del whole
        total = stem[...].astype(bf16).astype(f32) + right[right.shape[0] - stem.shape[0] :, :].astype(f32)
        for k in range(stem_out.shape[0]):
            stem_out[k] = total[4 * k : 4 * k + 4, :]
    else:
        out, room, sems = rest
    bits = [piece_bits(flip, 1, 0), piece_bits(flip, 0, 1)]
    copies_at = sizes[0] * 4 // unit
    place_units([left], sizes[:1], offsets[:1], unit, size, bits[0], out, room.at[pl.ds(0, sizes[0] * 4)], sems.at[pl.ds(0, copies_at)])
    place_units([right], sizes[1:], offsets[1:], unit, size, bits[1], out, room.at[pl.ds(sizes[0] * 4, sizes[1] * 4)], sems.at[pl.ds(copies_at, sizes[1] * 4 // unit)])


def per_device(codes, variant_pos, variant_shift, stem_weight, conv_weight, cotangent):
    n_dp, n_ctx = lax.axis_size("dp"), lax.axis_size("context")
    devices = n_dp * n_ctx
    length = codes.shape[1]
    rows = length // 2
    taps, _, width = stem_weight.shape
    half = width // 2
    total = rows * n_ctx
    lanes = -(-(rows + 256) // 128) * 128
    ctx = lax.axis_index("context")
    core = ctx % 2
    cot = cotangent[0]
    x_bit, y_bit = 2, n_ctx

    def swap(value, even_bit, odd_bit=None):
        odd_bit = even_bit if odd_bit is None else odd_bit
        pairs = [(i, i ^ (odd_bit if i & 1 else even_bit)) for i in range(devices)]
        return lax.ppermute(value, AXES, pairs)

    outward = []
    for d in range(n_dp):
        for c in range(n_ctx):
            other = c + 1 if c & 1 else c - 1
            if 0 <= other < n_ctx:
                outward.append((d * n_ctx + c, d * n_ctx + other))

    edge = jax.ShapeDtypeStruct((16, lanes), bf16)
    message = jax.ShapeDtypeStruct((rows + 16, width), bf16)
    own, near, far, msg = pl.pallas_call(
        functools.partial(first_kernel, rows, lanes),
        out_shape=[edge, edge, edge, message],
        in_specs=[FAR] * 4,
        out_specs=[VMEM] * 4,
        scratch_shapes=[
            pltpu.VMEM((1, length), jnp.int32),
            pltpu.SMEM(variant_pos.shape, jnp.int32),
            pltpu.SMEM(variant_pos.shape, jnp.int32),
            pltpu.VMEM((16, width), bf16),
            pltpu.VMEM((16, width), bf16),
            pltpu.SemaphoreType.DMA((6,)),
        ],
        compiler_params=params(),
    )(codes, variant_pos, variant_shift, cot)
    near = swap(near, 1)
    msg = pl.pallas_call(
        message_kernel,
        grid=(1,),
        out_shape=message,
        in_specs=[
            pl.BlockSpec((16, lanes), lambda i: (0, 0)),
            pl.BlockSpec((16, lanes), lambda i: (0, 0)),
            pl.BlockSpec(memory_space=pl.ANY),
        ],
        out_specs=pl.BlockSpec((16, width), lambda i: (rows // 16, 0)),
        input_output_aliases={2: 0},
        compiler_params=params(),
    )(own, near, msg)
    msg = swap(msg, y_bit)
    outer = far
    far = lax.ppermute(outer, AXES, outward)
    pair_far = lax.ppermute(outer, AXES, [(a, b ^ y_bit) for a, b in outward])

    weight, half_weight = pl.pallas_call(
        weight_kernel,
        out_shape=[
            jax.ShapeDtypeStruct((192, 2 * width), bf16),
            jax.ShapeDtypeStruct((192, width), bf16),
        ],
        in_specs=[VMEM],
        out_specs=[VMEM] * 2,
        compiler_params=params(),
    )(stem_weight)

    gates = [
        pltpu.VMEM((width, rows + 128), f32),
        pltpu.VMEM((TAPS * half, rows), bf16),
    ]
    part = pl.pallas_call(
        functools.partial(own_kernel, rows, total),
        out_shape=jax.ShapeDtypeStruct((TAPS * half, width), f32),
        in_specs=[VMEM] * 4 + [FAR],
        out_specs=VMEM,
        scratch_shapes=gates + [pltpu.VMEM((rows, width), bf16), pltpu.SemaphoreType.DMA],
        compiler_params=params(),
    )(own, near, far, half_weight, cot)

    size = TAPS * half // 2
    sent, kept = pl.pallas_call(
        functools.partial(pair_kernel, rows, total),
        out_shape=[
            jax.ShapeDtypeStruct((size, width), bf16),
            jax.ShapeDtypeStruct((size, width), f32),
        ],
        in_specs=[VMEM] * 4,
        out_specs=[VMEM] * 2,
        scratch_shapes=gates,
        compiler_params=params(),
    )(part, msg, pair_far, half_weight)
    value = kept + swap(sent, 1).astype(f32)
    x = ctx // x_bit % 2
    size //= 2
    sent = lax.dynamic_slice_in_dim(value, (1 - x) * size, size, 0).astype(bf16)
    kept = lax.dynamic_slice_in_dim(value, x * size, size, 0)
    value = kept + swap(sent, x_bit).astype(f32)

    padded = rows + 2 * LEAD
    cost = pl.CostEstimate(
        flops=2 * TAPS * rows * width * width, bytes_accessed=4 << 20, transcendentals=0
    )
    d_pooled, stem_part, gated, pooled = pl.pallas_call(
        functools.partial(back_kernel, rows, total),
        out_shape=[
            jax.ShapeDtypeStruct((rows, width), bf16),
            jax.ShapeDtypeStruct((4 * taps + 4, width), f32),
            jax.ShapeDtypeStruct((padded, width), bf16),
            jax.ShapeDtypeStruct((rows, width), bf16),
        ],
        in_specs=[VMEM] * 4 + [FAR] * 2,
        out_specs=[VMEM] * 4,
        scratch_shapes=[
            pltpu.VMEM((padded, 2 * width), f32),
            pltpu.VMEM((padded, width), bf16),
            pltpu.VMEM((rows, width), f32),
            pltpu.VMEM(conv_weight.shape, bf16),
            pltpu.VMEM((rows, width), bf16),
            pltpu.SemaphoreType.DMA((2,)),
        ],
        compiler_params=params(),
        cost_estimate=cost,
    )(after(own, sent), near, far, weight, conv_weight, cot)

    unit = half // 4
    cut = 3 * unit
    left = value[:cut]
    right = jnp.concatenate([value[cut:], stem_part], axis=0)
    others = [1 << k for k in range(devices.bit_length() - 1) if (1 << k) not in (1, x_bit, y_bit)]
    last = None
    for b in others:
        left, right = rounded(left), rounded(right)
        last = left
        left, right = [v + swap(v.astype(bf16), b).astype(f32) for v in (left, right)]
    features = pl.pallas_call(
        functools.partial(feature_kernel, rows),
        out_shape=jax.ShapeDtypeStruct((rows, width), bf16),
        in_specs=[VMEM] * 2 + [FAR],
        out_specs=VMEM,
        scratch_shapes=[pltpu.VMEM(conv_weight.shape, bf16), pltpu.SemaphoreType.DMA],
        compiler_params=params(),
        cost_estimate=cost,
    )(gated, after(pooled, last), conv_weight)

    rest = size - cut
    left = left.astype(bf16)
    stem_sum = right[rest:]
    right = right[:rest].astype(bf16)
    for one, two in ((x_bit, y_bit), (y_bit, x_bit)):
        got = swap(left, one, two)
        left = jnp.concatenate([left, got], axis=0)
        stem_sum = rounded(stem_sum)
        got = swap(jnp.concatenate([right, stem_sum.astype(bf16)], axis=0), two, one)
        stem_sum = stem_sum + got[right.shape[0] :].astype(f32)
        right = jnp.concatenate([right, got[: right.shape[0]]], axis=0)
    got_left = swap(left, 1)
    got_right = swap(jnp.concatenate([right, stem_sum.astype(bf16)], axis=0), 1)

    sizes, offsets = (cut, rest), (0, cut)
    whole = jax.ShapeDtypeStruct((TAPS * width, width), f32)
    room = [pltpu.VMEM((4 * size, width), f32), pltpu.SemaphoreType.DMA((4 * size // unit,))]
    conv_grad = pl.pallas_call(
        functools.partial(place_kernel, 0, sizes, offsets, unit, size),
        out_shape=whole,
        in_specs=[VMEM] * 2,
        out_specs=FAR,
        scratch_shapes=room,
        compiler_params=params(),
        cost_estimate=pl.CostEstimate(flops=0, bytes_accessed=4 << 20, transcendentals=0),
    )(left, right)
    conv_grad, stem_grad = pl.pallas_call(
        functools.partial(place_kernel, 1, sizes, offsets, unit, size),
        out_shape=[whole, jax.ShapeDtypeStruct(stem_weight.shape, f32)],
        in_specs=[VMEM] * 3 + [FAR],
        out_specs=[FAR, VMEM],
        scratch_shapes=room,
        input_output_aliases={3: 0},
        compiler_params=params(),
    )(got_left, got_right, stem_sum, conv_grad)
    conv_grad = conv_grad.reshape(TAPS, width, width)
    return (features[None], d_pooled[None], conv_grad, stem_grad)


def solution(mesh):
    placed = (P("dp", "context"), P("dp", None), P("dp", None), P(), P(), P("dp", "context", None))
    return jax.shard_map(
        per_device,
        mesh=mesh,
        in_specs=placed,
        out_specs=(P("dp", "context", None), P("dp", "context", None), P(), P()),
        check_vma=False,
    )
```

```python
import functools
import math

import jax
import jax.numpy as jnp
from jax import lax
from jax.experimental import pallas as pl
from jax.experimental.pallas import tpu as pltpu
from jax.sharding import PartitionSpec as P

root_scale = math.sqrt(2.0 / math.pi)
cubic = 0.044715
AXES = ("dp", "context")
TAPS = 5
FIRST = 3
FIRST_LIMIT = 48
HALO = 6
LEAD = 16
VMEM = pl.BlockSpec(memory_space=pltpu.VMEM)
FAR = pl.BlockSpec(memory_space=pltpu.HBM)
bf16 = jnp.bfloat16
f32 = jnp.float32


def gelu_tanh(value):
    inner = jnp.tanh(value * (root_scale + (root_scale * cubic) * (value * value)))
    half = 0.5 * value
    return half + half * inner


def gelu_both(value):
    square = value * value
    inner = jnp.tanh(value * (root_scale + (root_scale * cubic) * square))
    rise = (1.0 - inner * inner) * (root_scale + (3.0 * root_scale * cubic) * square)
    half = 0.5 * value
    return half + half * inner, 0.5 + 0.5 * inner + half * rise


def rounded(value):
    return lax.reduce_precision(value, 8, 7)


def params(limit=24):
    return pltpu.CompilerParams(vmem_limit_bytes=limit * 1024 * 1024)


def together(*values):
    return lax.optimization_barrier(values)


def after(value, *others):
    return together(value, *others)[0]


def first_kernel(
    rows,
    lanes,
    codes,
    positions,
    amounts,
    cot,
    stem_weight,
    own,
    near,
    far,
    weight,
    half_weight,
    base_v,
    pos_s,
    amt_s,
    top,
    bottom,
    weight_v,
    sems,
):
    length = 2 * rows
    tiles = length // 128
    width = cot.shape[1]
    copies = [
        pltpu.make_async_copy(codes, base_v, sems.at[0]),
        pltpu.make_async_copy(positions, pos_s, sems.at[1]),
        pltpu.make_async_copy(amounts, amt_s, sems.at[2]),
        pltpu.make_async_copy(cot.at[pl.ds(0, 16)], top, sems.at[3]),
        pltpu.make_async_copy(cot.at[pl.ds(rows - 16, 16)], bottom, sems.at[4]),
        pltpu.make_async_copy(stem_weight, weight_v, sems.at[5]),
    ]
    for copy in copies:
        copy.start()
    ctx = lax.axis_index("context")
    core = lax.rem(ctx, 2)
    for copy in copies[:5]:
        copy.wait()
    x = jnp.concatenate([base_v[:, 128 * q : 128 * q + 128] for q in range(tiles)], axis=0)
    spot = (
        ctx * length
        + 128 * lax.broadcasted_iota(jnp.int32, x.shape, 0)
        + lax.broadcasted_iota(jnp.int32, x.shape, 1)
    )
    sums = [x] + [jnp.zeros_like(x)] * 3
    for v in range(positions.shape[1]):
        sums[v % 4] = sums[v % 4] + jnp.where(spot == pos_s[0, v], amt_s[0, v], 0)
    x = (sums[0] + sums[1]) + (sums[2] + sums[3])
    x = ((x & 3) + 1).astype(f32).astype(bf16)
    source = lax.broadcasted_iota(jnp.int32, (128, 128), 0)
    target = lax.broadcasted_iota(jnp.int32, (128, 128), 1)

    def picked(parity):
        left = (source == 2 * target + parity).astype(f32).astype(bf16)
        right = (source == 2 * (target - 64) + parity).astype(f32).astype(bf16)
        low = jnp.dot(x, left, preferred_element_type=f32)
        high = jnp.dot(x, right, preferred_element_type=f32)
        parts = [low[2 * q : 2 * q + 1] + high[2 * q + 1 : 2 * q + 2] for q in range(tiles // 2)]
        return jnp.concatenate(parts + [jnp.zeros((1, lanes - rows), f32)], axis=1)

    both = jnp.concatenate([picked(0), picked(1), jnp.zeros((6, lanes), f32)], axis=0)
    lane = lax.broadcasted_iota(jnp.int32, both.shape, 1)
    shifted = pltpu.roll(both, HALO, 1)
    last = jnp.where(lane < HALO, pltpu.roll(both, lanes - (rows - HALO), 1), 0.0)
    ahead = (lane >= rows + HALO) & (lane < rows + 2 * HALO)
    first = jnp.where(ahead, pltpu.roll(both, rows + HALO, 1), 0.0)
    blank = jnp.zeros((8, lanes), f32)
    pad = jnp.zeros((2, lanes - width), f32)

    def message(edge, grads):
        grads = jnp.concatenate([grads, pad], axis=1)
        return jnp.concatenate([edge, grads, jnp.zeros((6, lanes), f32)], axis=0)

    head = message(first, top[...].astype(f32)[0:2])
    tail = message(last, bottom[...].astype(f32)[14:16])
    own[...] = jnp.concatenate([shifted, blank], axis=0).astype(bf16)
    near[...] = jnp.where(core == 0, tail, head).astype(bf16)
    far[...] = jnp.where(core == 0, head, tail).astype(bf16)
    copies[5].wait()
    stem_terms(weight_v, weight, half_weight)


def stem_terms(weight, out, half_out):
    width = weight.shape[2]
    zero = jnp.zeros((1, width), f32)
    even, odd = orders(weight.shape[0])

    def rows(order):
        return jnp.concatenate(
            [
                zero if k is None else weight[k, a : a + 1, :]
                for a in range(4)
                for k in order
            ],
            axis=0,
        )

    def terms(full):
        high = full.astype(bf16)
        left = full - high.astype(f32)
        middle = left.astype(bf16)
        low = (left - middle.astype(f32)).astype(bf16)
        return jnp.concatenate([high, middle, low], axis=0)

    evens, odds = rows(even), rows(odd)
    half = width // 2
    upper = lax.rem(lax.axis_index("dp"), 2) == 1
    out[...] = terms(jnp.concatenate([evens, odds], axis=1))
    mine = [jnp.where(upper, v[:, half:], v[:, :half]) for v in (evens, odds)]
    half_out[...] = terms(jnp.concatenate(mine, axis=1))


def orders(taps):
    even = [None] + list(range(taps - 2, 0, -2)) + list(range(taps - 1, -1, -2))
    odd = list(range(taps - 1, -1, -2)) + list(range(taps - 2, 0, -2)) + [None]
    return even, odd


def one_hot(codes, lanes, shift):
    even = jnp.broadcast_to(codes[0:1], (8, lanes))
    odd = jnp.broadcast_to(codes[1:2], (8, lanes))
    even = pltpu.roll(even, (2 * lanes - 8 + shift) % lanes, 1, stride=1, stride_axis=0)
    odd = pltpu.roll(odd, (2 * lanes - 7 + shift) % lanes, 1, stride=1, stride_axis=0)
    near = jnp.concatenate([even, odd], axis=0)
    return jnp.concatenate([(near == a + 1.0).astype(f32) for a in range(4)], axis=0).astype(bf16)


def shifted_gates(codes, first, total, weight, rows, stem, gated):
    used = rows + 128
    half = weight.shape[1] // 2
    quarter = half // 4
    hot = one_hot(codes, codes.shape[1], 0)[:, :used]
    hot = jnp.concatenate([hot, hot, hot], axis=0)
    stem[...] = lax.dot_general(
        weight[...], hot, (((0,), (0,)), ((), ())), preferred_element_type=f32
    )
    spot = first - 2 + lax.broadcasted_iota(jnp.int32, (1, used), 1)
    inside = (spot >= 0) & (spot < total)
    step = 16
    for c in range(0, half, step):
        even = gelu_tanh(stem[c : c + step, :])
        odd = gelu_tanh(stem[half + c : half + c + step, :])
        pooled = (0.5 * (even + odd)).astype(bf16).astype(f32)
        value = jnp.where(inside, gelu_tanh(pooled), 0.0)
        for t in range(TAPS):
            moved = value if t == 0 else pltpu.roll(value, used - t, 1)
            at = (c // quarter * TAPS + t) * quarter + c % quarter
            gated[at : at + step, :] = moved[:, :rows].astype(bf16)


def own_kernel(rows, total, own, near, far, weight, cot, out, stem, gated, cot_v, sem):
    copy = pltpu.make_async_copy(cot, cot_v, sem)
    copy.start()
    first = lax.axis_index("context") * rows
    codes = (own[...].astype(f32) + near[...].astype(f32) + far[...].astype(f32))[0:8]
    shifted_gates(codes, first, total, weight, rows, stem, gated)
    copy.wait()
    out[...] = jnp.dot(gated[...], cot_v[...], preferred_element_type=f32)


def pair_kernel(rows, total, codes, weight, gated, stem):
    first = lax.axis_index("context") * rows
    shifted_gates(codes[...].astype(f32)[0:8], first, total, weight, rows, stem, gated)


def sum_kernel(part, gated, cot, sent, kept):
    core = lax.rem(lax.axis_index("context"), 2)
    size = sent.shape[0]
    for which, out in ((1 - core, sent), (core, kept)):
        span = pl.ds(pl.multiple_of(which * size, 16), size)
        value = part[span, :] + jnp.dot(gated[span, :], cot[...], preferred_element_type=f32)
        out[...] = value.astype(out.dtype)


def split_kernel(value, got, sent, kept):
    x = lax.rem(lax.axis_index("context") // 2, 2)
    size = sent.shape[0]
    for which, out in ((1 - x, sent), (x, kept)):
        span = pl.ds(pl.multiple_of(which * size, 16), size)
        out[...] = (value[span, :] + got[span, :].astype(f32)).astype(out.dtype)


def back_kernel(rows, conv, cot, back, ext, sem):
    width = cot.shape[1]
    copy = pltpu.make_async_copy(cot, ext.at[pl.ds(LEAD, rows)], sem)
    copy.start()
    blank = jnp.zeros((LEAD, width), bf16)
    ext[0:LEAD, :] = blank
    ext[LEAD + rows :, :] = blank
    copy.wait()
    for t in range(TAPS):
        start = LEAD + 2 - t
        term = turned(ext[start : start + rows, :], conv[t])
        back[...] = term if t == 0 else back[...] + term


def turned(left, right):
    return lax.dot_general(left, right, (((1,), (1,)), ((), ())), preferred_element_type=f32)


def edge_terms(near, far, conv):
    width = conv.shape[1]
    core = lax.rem(lax.axis_index("context"), 2)
    near_v, far_v = near[...].astype(f32), far[...].astype(f32)
    before = jnp.where(core == 0, far_v, near_v)[8:10, :width]
    behind = jnp.where(core == 0, near_v, far_v)[8:10, :width]
    none = jnp.zeros((6, width), f32)
    one = jnp.zeros((1, width), f32)
    top = jnp.concatenate([before, none], axis=0).astype(bf16)
    top_late = jnp.concatenate([before[1:2], one, none], axis=0).astype(bf16)
    end = jnp.concatenate([none, behind], axis=0).astype(bf16)
    end_late = jnp.concatenate([none, one, behind[0:1]], axis=0).astype(bf16)
    first = turned(top, conv[4]) + turned(top_late, conv[3])
    last = turned(end, conv[0]) + turned(end_late, conv[1])
    return first, last


def slope_kernel(
    rows, total, own, near, far, weight, back, conv, cot, d_pooled, stem_part, gated, pooled, stem, cot_v, sem
):
    copy = pltpu.make_async_copy(cot, cot_v, sem)
    copy.start()
    lanes = own.shape[1]
    width = cot.shape[1]
    padded = rows + 2 * LEAD
    codes = (own[...].astype(f32) + near[...].astype(f32) + far[...].astype(f32))[0:8]
    hot = one_hot(codes, lanes, LEAD - 2)[:, :padded]
    hot = jnp.concatenate([hot, hot, hot], axis=0)
    stem[...] = lax.dot_general(
        hot, weight[...], (((0,), (0,)), ((), ())), preferred_element_type=f32
    )
    mine = one_hot(codes, lanes, lanes - 2)
    first = lax.axis_index("context") * rows
    for edge in (0, LEAD + rows):
        act = 0.5 * (
            gelu_tanh(stem[edge : edge + LEAD, :width]) + gelu_tanh(stem[edge : edge + LEAD, width:])
        )
        act = act.astype(bf16).astype(f32)
        spot = first - LEAD + edge + lax.broadcasted_iota(jnp.int32, (LEAD, 1), 0)
        inside = (spot >= 0) & (spot < total)
        gated[edge : edge + LEAD, :] = jnp.where(inside, gelu_tanh(act), 0.0).astype(bf16)
    top, end = edge_terms(near, far, conv)
    none = jnp.zeros((24, width), f32)
    copy.wait()
    step = 32
    for r in range(0, rows, step):
        even = stem[LEAD + r : LEAD + r + step, :width]
        odd = stem[LEAD + r : LEAD + r + step, width:]
        even, even_slope = gelu_both(even)
        odd, odd_slope = gelu_both(odd)
        low = (0.5 * (even + odd)).astype(bf16)
        pooled[r : r + step, :] = low
        gate, slope = gelu_both(low.astype(f32))
        gated[LEAD + r : LEAD + r + step, :] = gate.astype(bf16)
        rise = back[r : r + step, :]
        if r == 0:
            rise = rise + jnp.concatenate([top, none], axis=0)
        if r + step == rows:
            rise = rise + jnp.concatenate([none, end], axis=0)
        grad = cot_v[r : r + step, :].astype(f32) + rise * slope
        d_pooled[r : r + step, :] = grad.astype(bf16)
        half = 0.5 * grad
        stem[LEAD + r : LEAD + r + step, :width] = half * even_slope
        stem[LEAD + r : LEAD + r + step, width:] = half * odd_slope
    grads = jnp.dot(
        mine[:, :rows], stem[LEAD : LEAD + rows, :].astype(bf16), preferred_element_type=f32
    )
    even, odd = orders(stem_part.shape[0] // 4 - 1)
    for k in range(len(even) - 1):
        for a in range(4):
            p, q = 16 * a + even.index(k), 16 * a + odd.index(k)
            stem_part[4 * k + a : 4 * k + a + 1, :] = (
                grads[p : p + 1, :width] + grads[q : q + 1, width:]
            )
    stem_part[stem_part.shape[0] - 4 :, :] = jnp.zeros((4, width), f32)


def feature_kernel(rows, gated, pooled, conv, out):
    acc = pooled[...].astype(f32)
    for t in range(TAPS):
        start = LEAD - 2 + t
        acc = acc + jnp.dot(gated[start : start + rows, :], conv[t], preferred_element_type=f32)
    out[...] = acc.astype(bf16)


def put_pieces(flip, chains, out, room, sems):
    ctx = lax.axis_index("context")
    core = lax.rem(ctx, 2)
    x = lax.rem(ctx // 2, 2)
    y = lax.rem(lax.axis_index("dp"), 2)
    unit = room.shape[1]
    half = out.shape[1] // 2
    from_core = lax.rem(core + flip, 2)
    copies = []
    at = 0
    for chain, (piece, tap, taps) in enumerate(chains):
        x_first = jnp.where(from_core == chain, 1, 0)
        for p in range(4):
            one, two = p % 2, p // 2
            dx = jnp.where(x_first == 1, one, two)
            dy = one + two - dx
            from_x, from_y = lax.rem(x + dx, 2), lax.rem(y + dy, 2)
            channel = from_y * half + (2 * from_core + from_x) * unit
            for t in range(taps):
                low = (p * taps + t) * unit
                room[at + t] = piece[low : low + unit, :].astype(f32)
            copy = pltpu.make_async_copy(
                room.at[pl.ds(at, taps)],
                out.at[pl.ds(tap, taps), pl.ds(pl.multiple_of(channel, 16), unit)],
                sems.at[len(copies)],
            )
            copy.start()
            copies.append(copy)
            at += taps
    return copies


def place_kernel(left, right, out, room, sems):
    for copy in put_pieces(0, ((left, 0, FIRST), (right, FIRST, TAPS - FIRST)), out, room, sems):
        copy.wait()


def last_kernel(left, right, stem, whole, out, stem_out, room, sems):
    del whole
    copies = put_pieces(
        1, ((left, 0, FIRST), (right, FIRST, TAPS - FIRST)), out, room, sems
    )
    core = lax.rem(lax.axis_index("context"), 2)
    mine = stem[...].astype(bf16).astype(f32)
    other = right[right.shape[0] - stem.shape[0] :, :].astype(f32)
    whole_stem = jnp.concatenate(
        [jnp.where(core == 0, mine, other), jnp.where(core == 0, other, mine)], axis=0
    )
    for k in range(stem_out.shape[0]):
        stem_out[k] = whole_stem[4 * k : 4 * k + 4, :]
    for copy in copies:
        copy.wait()


def per_device(codes, variant_pos, variant_shift, stem_weight, conv_weight, cotangent):
    n_dp, n_ctx = lax.axis_size("dp"), lax.axis_size("context")
    devices = n_dp * n_ctx
    length = codes.shape[1]
    rows = length // 2
    taps, _, width = stem_weight.shape
    half = width // 2
    unit = half // 4
    total = rows * n_ctx
    lanes = -(-(rows + 256) // 128) * 128
    core = lax.axis_index("context") % 2
    cot = cotangent[0]
    x_bit, y_bit = 2, n_ctx

    def swap(value, even_bit, odd_bit=None):
        odd_bit = even_bit if odd_bit is None else odd_bit
        pairs = [(i, i ^ (odd_bit if i & 1 else even_bit)) for i in range(devices)]
        return lax.ppermute(value, AXES, pairs)

    def call(kernel, out, operands, scratch=(), **options):
        shapes = [jax.ShapeDtypeStruct(o[0], o[1]) for o in out]
        specs = [o[2] if len(o) > 2 else VMEM for o in out]
        options.setdefault("compiler_params", params())
        return pl.pallas_call(
            kernel,
            out_shape=shapes,
            in_specs=[spec for _, spec in operands],
            out_specs=specs,
            scratch_shapes=list(scratch),
            **options,
        )(*[value for value, _ in operands])

    def near_by(*values):
        return [(value, VMEM) for value in values]

    def far_off(*values):
        return [(pltpu.with_memory_space_constraint(value, pltpu.HBM), FAR) for value in values]

    outward = {}
    for d in range(n_dp):
        for c in range(n_ctx):
            other = c + 1 if c & 1 else c - 1
            if 0 <= other < n_ctx:
                outward[d * n_ctx + c] = d * n_ctx + other

    pair_cot = swap(cot, y_bit)
    dma = pltpu.SemaphoreType.DMA
    edge = ((16, lanes), bf16)
    own, near, far, weight, half_weight = call(
        functools.partial(first_kernel, rows, lanes),
        [edge, edge, edge, ((192, 2 * width), bf16), ((192, width), bf16)],
        far_off(codes, variant_pos, variant_shift, cot, stem_weight),
        [
            pltpu.VMEM((1, length), jnp.int32),
            pltpu.SMEM(variant_pos.shape, jnp.int32),
            pltpu.SMEM(variant_pos.shape, jnp.int32),
            pltpu.VMEM((16, width), bf16),
            pltpu.VMEM((16, width), bf16),
            pltpu.VMEM(stem_weight.shape, f32),
            dma((6,)),
        ],
        compiler_params=params(FIRST_LIMIT),
    )
    near = swap(near, 1)
    cost = pl.CostEstimate(
        flops=2 * TAPS * rows * width * width, bytes_accessed=4 << 20, transcendentals=0
    )
    padded = rows + 2 * LEAD
    (back,) = call(
        functools.partial(back_kernel, rows),
        [((rows, width), f32)],
        near_by(conv_weight) + far_off(after(cot, far)),
        [pltpu.VMEM((padded, width), bf16), dma],
        cost_estimate=cost,
    )
    far = lax.ppermute(far, AXES, list(outward.items()))
    pair_codes = swap(own + near + far, y_bit)
    stem_half = pltpu.VMEM((width, rows + 128), f32)
    gates = ((TAPS * half, rows), bf16)
    (part,) = call(
        functools.partial(own_kernel, rows, total),
        [((TAPS * half, width), f32)],
        near_by(own, near, far, half_weight) + far_off(cot),
        [stem_half, pltpu.VMEM(*gates), pltpu.VMEM((rows, width), bf16), dma],
    )
    (pair_gates,) = call(
        functools.partial(pair_kernel, rows, total),
        [gates],
        near_by(pair_codes, half_weight),
        [stem_half],
    )
    size = TAPS * half // 2
    sent, kept = call(
        sum_kernel, [((size, width), bf16), ((size, width), f32)], near_by(part, pair_gates, pair_cot)
    )
    got = swap(sent, 1)
    size //= 2
    sent, kept = call(
        split_kernel, [((size, width), bf16), ((size, width), f32)], near_by(kept, got)
    )
    got = swap(sent, x_bit)
    d_pooled, stem_part, gated, pooled = call(
        functools.partial(slope_kernel, rows, total),
        [
            ((rows, width), bf16),
            ((4 * taps + 4, width), f32),
            ((padded, width), bf16),
            ((rows, width), bf16),
        ],
        near_by(after(own, sent), near, far, weight, back, conv_weight) + far_off(cot),
        [pltpu.VMEM((padded, 2 * width), f32), pltpu.VMEM((rows, width), bf16), dma],
        cost_estimate=cost,
    )
    value = kept + got.astype(f32)

    few = stem_part.shape[0] // 2
    stem_part = after(stem_part, value)
    stem_got = swap(lax.dynamic_slice_in_dim(stem_part, (1 - core) * few, few, 0).astype(bf16), 1)
    stem_sum = lax.dynamic_slice_in_dim(stem_part, core * few, few, 0) + stem_got.astype(f32)

    cut = FIRST * unit
    rest = size - cut
    left = value[:cut]
    right = jnp.concatenate([value[cut:], stem_sum], axis=0)
    others = [1 << k for k in range(devices.bit_length() - 1) if (1 << k) not in (1, x_bit, y_bit)]
    for k, b in enumerate(others):
        odd_b = others[(k + 1) % len(others)]
        left, right = rounded(left), rounded(right)
        if k == len(others) - 1:
            pooled = after(pooled, right)
        left, right = [v + swap(v.astype(bf16), b, odd_b).astype(f32) for v in (left, right)]
    (features,) = call(
        functools.partial(feature_kernel, rows),
        [((rows, width), bf16)],
        near_by(gated, pooled, conv_weight),
        cost_estimate=cost,
    )
    left, features = together(left, features)
    left = left.astype(bf16)
    stem_sum = right[rest:]
    right = right[:rest].astype(bf16)

    whole = ((TAPS, width, width), f32, FAR)

    for one, two in ((x_bit, y_bit), (y_bit, x_bit)):
        got_left = swap(left, one, two)
        stem_sum = rounded(stem_sum)
        got_right = swap(jnp.concatenate([right, stem_sum.astype(bf16)], axis=0), two, one)
        stem_sum = stem_sum + got_right[right.shape[0] :].astype(f32)
        left = jnp.concatenate([left, got_left], axis=0)
        right = jnp.concatenate([right, got_right[: right.shape[0]]], axis=0)
    got_left = swap(left, 1)
    got_right = swap(jnp.concatenate([right, stem_sum.astype(bf16)], axis=0), 1)
    (conv_grad,) = call(
        place_kernel,
        [whole],
        near_by(left, right),
        [pltpu.VMEM((TAPS * 4, unit, width), f32), dma((8,))],
    )
    conv_grad, stem_grad = call(
        last_kernel,
        [whole, (stem_weight.shape, f32)],
        near_by(got_left, got_right, stem_sum) + far_off(conv_grad),
        [pltpu.VMEM((TAPS * 4, unit, width), f32), dma((8,))],
        input_output_aliases={3: 0},
    )
    return (features[None], d_pooled[None], conv_grad, stem_grad)


def solution(mesh):
    placed = (P("dp", "context"), P("dp", None), P("dp", None), P(), P(), P("dp", "context", None))
    return jax.shard_map(
        per_device,
        mesh=mesh,
        in_specs=placed,
        out_specs=(P("dp", "context", None), P("dp", "context", None), P(), P()),
        check_vma=False,
    )
```

```python
import functools
import math

import jax
import jax.numpy as jnp
from jax import lax
from jax.experimental import pallas as pl
from jax.experimental.pallas import tpu as pltpu
from jax.sharding import PartitionSpec as P

root_scale = math.sqrt(2.0 / math.pi)
cubic = 0.044715
AXES = ("dp", "context")
TAPS = 5
FIRST = 3
FIRST_LIMIT = 48
HALO = 6
LEAD = 16
VMEM = pl.BlockSpec(memory_space=pltpu.VMEM)
FAR = pl.BlockSpec(memory_space=pltpu.HBM)
bf16 = jnp.bfloat16
f32 = jnp.float32


def gelu_tanh(value):
    inner = jnp.tanh(value * (root_scale + (root_scale * cubic) * (value * value)))
    half = 0.5 * value
    return half + half * inner


def gelu_both(value):
    square = value * value
    inner = jnp.tanh(value * (root_scale + (root_scale * cubic) * square))
    rise = (1.0 - inner * inner) * (root_scale + (3.0 * root_scale * cubic) * square)
    half = 0.5 * value
    return half + half * inner, 0.5 + 0.5 * inner + half * rise


def rounded(value):
    return lax.reduce_precision(value, 8, 7)


def params(limit=24):
    return pltpu.CompilerParams(vmem_limit_bytes=limit * 1024 * 1024)


def together(*values):
    return lax.optimization_barrier(values)


def after(value, *others):
    return together(value, *others)[0]


def holding(kernel, operands, results, kept):
    def run(*refs):
        last = operands + kept + results
        kernel(*refs[:operands], *refs[operands + kept : last], *refs[last + kept :])

    return run


def first_kernel(
    rows,
    lanes,
    codes,
    positions,
    amounts,
    cot,
    stem_weight,
    conv,
    own,
    near,
    far,
    weight,
    half_weight,
    cot_out,
    conv_out,
    base_v,
    pos_s,
    amt_s,
    weight_v,
    sems,
):
    length = 2 * rows
    tiles = length // 128
    width = cot.shape[1]
    copies = [
        pltpu.make_async_copy(codes, base_v, sems.at[0]),
        pltpu.make_async_copy(positions, pos_s, sems.at[1]),
        pltpu.make_async_copy(amounts, amt_s, sems.at[2]),
        pltpu.make_async_copy(cot, cot_out, sems.at[3]),
        pltpu.make_async_copy(stem_weight, weight_v, sems.at[4]),
        pltpu.make_async_copy(conv, conv_out, sems.at[5]),
    ]
    for copy in copies:
        copy.start()
    ctx = lax.axis_index("context")
    core = lax.rem(ctx, 2)
    for copy in copies[:4]:
        copy.wait()
    x = jnp.concatenate([base_v[:, 128 * q : 128 * q + 128] for q in range(tiles)], axis=0)
    spot = (
        ctx * length
        + 128 * lax.broadcasted_iota(jnp.int32, x.shape, 0)
        + lax.broadcasted_iota(jnp.int32, x.shape, 1)
    )
    sums = [x] + [jnp.zeros_like(x)] * 3
    for v in range(positions.shape[1]):
        sums[v % 4] = sums[v % 4] + jnp.where(spot == pos_s[0, v], amt_s[0, v], 0)
    x = (sums[0] + sums[1]) + (sums[2] + sums[3])
    x = ((x & 3) + 1).astype(f32).astype(bf16)
    source = lax.broadcasted_iota(jnp.int32, (128, 128), 0)
    target = lax.broadcasted_iota(jnp.int32, (128, 128), 1)

    def picked(parity):
        left = (source == 2 * target + parity).astype(f32).astype(bf16)
        right = (source == 2 * (target - 64) + parity).astype(f32).astype(bf16)
        low = jnp.dot(x, left, preferred_element_type=f32)
        high = jnp.dot(x, right, preferred_element_type=f32)
        parts = [low[2 * q : 2 * q + 1] + high[2 * q + 1 : 2 * q + 2] for q in range(tiles // 2)]
        return jnp.concatenate(parts + [jnp.zeros((1, lanes - rows), f32)], axis=1)

    both = jnp.concatenate([picked(0), picked(1), jnp.zeros((6, lanes), f32)], axis=0)
    lane = lax.broadcasted_iota(jnp.int32, both.shape, 1)
    shifted = pltpu.roll(both, HALO, 1)
    last = jnp.where(lane < HALO, pltpu.roll(both, lanes - (rows - HALO), 1), 0.0)
    ahead = (lane >= rows + HALO) & (lane < rows + 2 * HALO)
    first = jnp.where(ahead, pltpu.roll(both, rows + HALO, 1), 0.0)
    blank = jnp.zeros((8, lanes), f32)
    pad = jnp.zeros((2, lanes - width), f32)

    def message(edge, grads):
        grads = jnp.concatenate([grads, pad], axis=1)
        return jnp.concatenate([edge, grads, jnp.zeros((6, lanes), f32)], axis=0)

    head = message(first, cot_out[0:16, :].astype(f32)[0:2])
    tail = message(last, cot_out[rows - 16 : rows, :].astype(f32)[14:16])
    own[...] = jnp.concatenate([shifted, blank], axis=0).astype(bf16)
    near[...] = jnp.where(core == 0, tail, head).astype(bf16)
    far[...] = jnp.where(core == 0, head, tail).astype(bf16)
    copies[4].wait()
    stem_terms(weight_v, weight, half_weight)
    copies[5].wait()


def stem_terms(weight, out, half_out):
    width = weight.shape[2]
    zero = jnp.zeros((1, width), f32)
    even, odd = orders(weight.shape[0])

    def rows(order):
        return jnp.concatenate(
            [
                zero if k is None else weight[k, a : a + 1, :]
                for a in range(4)
                for k in order
            ],
            axis=0,
        )

    def terms(full):
        high = full.astype(bf16)
        left = full - high.astype(f32)
        middle = left.astype(bf16)
        low = (left - middle.astype(f32)).astype(bf16)
        return jnp.concatenate([high, middle, low], axis=0)

    evens, odds = rows(even), rows(odd)
    half = width // 2
    upper = lax.rem(lax.axis_index("dp"), 2) == 1
    out[...] = terms(jnp.concatenate([evens, odds], axis=1))
    mine = [jnp.where(upper, v[:, half:], v[:, :half]) for v in (evens, odds)]
    half_out[...] = terms(jnp.concatenate(mine, axis=1))


def orders(taps):
    even = [None] + list(range(taps - 2, 0, -2)) + list(range(taps - 1, -1, -2))
    odd = list(range(taps - 1, -1, -2)) + list(range(taps - 2, 0, -2)) + [None]
    return even, odd


def one_hot(codes, lanes, shift):
    even = jnp.broadcast_to(codes[0:1], (8, lanes))
    odd = jnp.broadcast_to(codes[1:2], (8, lanes))
    even = pltpu.roll(even, (2 * lanes - 8 + shift) % lanes, 1, stride=1, stride_axis=0)
    odd = pltpu.roll(odd, (2 * lanes - 7 + shift) % lanes, 1, stride=1, stride_axis=0)
    near = jnp.concatenate([even, odd], axis=0)
    return jnp.concatenate([(near == a + 1.0).astype(f32) for a in range(4)], axis=0).astype(bf16)


def shifted_gates(codes, first, total, weight, rows, stem, gated):
    used = rows + 128
    half = weight.shape[1] // 2
    quarter = half // 4
    hot = one_hot(codes, codes.shape[1], 0)[:, :used]
    hot = jnp.concatenate([hot, hot, hot], axis=0)
    stem[...] = lax.dot_general(
        weight[...], hot, (((0,), (0,)), ((), ())), preferred_element_type=f32
    )
    spot = first - 2 + lax.broadcasted_iota(jnp.int32, (1, used), 1)
    inside = (spot >= 0) & (spot < total)
    step = 16
    for c in range(0, half, step):
        even = gelu_tanh(stem[c : c + step, :])
        odd = gelu_tanh(stem[half + c : half + c + step, :])
        pooled = (0.5 * (even + odd)).astype(bf16).astype(f32)
        value = jnp.where(inside, gelu_tanh(pooled), 0.0)
        for t in range(TAPS):
            moved = value if t == 0 else pltpu.roll(value, used - t, 1)
            at = (c // quarter * TAPS + t) * quarter + c % quarter
            gated[at : at + step, :] = moved[:, :rows].astype(bf16)


def own_kernel(rows, total, own, near, far, weight, conv, cot, out, edges, stem, gated):
    first = lax.axis_index("context") * rows
    codes = (own[...].astype(f32) + near[...].astype(f32) + far[...].astype(f32))[0:8]
    shifted_gates(codes, first, total, weight, rows, stem, gated)
    edges[...] = edge_terms(near, far, conv)
    out[...] = jnp.dot(gated[...], cot[...], preferred_element_type=f32)


def pair_kernel(rows, total, codes, weight, gated, stem):
    first = lax.axis_index("context") * rows
    shifted_gates(codes[...].astype(f32)[0:8], first, total, weight, rows, stem, gated)


def sum_kernel(part, gated, cot, sent, kept):
    core = lax.rem(lax.axis_index("context"), 2)
    size = sent.shape[0]
    for which, out in ((1 - core, sent), (core, kept)):
        span = pl.ds(pl.multiple_of(which * size, 16), size)
        value = part[span, :] + jnp.dot(gated[span, :], cot[...], preferred_element_type=f32)
        out[...] = value.astype(out.dtype)


def place_of():
    ctx = lax.axis_index("context")
    return ctx, lax.rem(ctx, 2), lax.rem(lax.axis_index("dp"), 2)


def quarter_bit(ctx, core):
    far = 4 if lax.axis_size("context") % 8 == 0 else 2
    return jnp.where(core == 0, lax.rem(ctx // 2, 2), lax.rem(ctx // far, 2))


def split_kernel(value, got, sent, kept):
    x = quarter_bit(*place_of()[:2])
    size = sent.shape[0]
    for which, out in ((1 - x, sent), (x, kept)):
        span = pl.ds(pl.multiple_of(which * size, 16), size)
        out[...] = (value[span, :] + got[span, :].astype(f32)).astype(out.dtype)


def back_kernel(rows, conv, cot, back, ext):
    width = cot.shape[1]
    blank = jnp.zeros((LEAD, width), bf16)
    ext[0:LEAD, :] = blank
    ext[LEAD : LEAD + rows, :] = cot[...]
    ext[LEAD + rows :, :] = blank
    for t in range(TAPS):
        start = LEAD + 2 - t
        term = turned(ext[start : start + rows, :], conv[t])
        back[...] = term if t == 0 else back[...] + term


def turned(left, right):
    return lax.dot_general(left, right, (((1,), (1,)), ((), ())), preferred_element_type=f32)


def edge_terms(near, far, conv):
    width = conv.shape[1]
    core = lax.rem(lax.axis_index("context"), 2)
    near_v, far_v = near[...].astype(f32), far[...].astype(f32)
    before = jnp.where(core == 0, far_v, near_v)[8:10, :width]
    behind = jnp.where(core == 0, near_v, far_v)[8:10, :width]
    none = jnp.zeros((6, width), f32)
    one = jnp.zeros((1, width), f32)
    top = jnp.concatenate([before, none], axis=0).astype(bf16)
    top_late = jnp.concatenate([before[1:2], one, none], axis=0).astype(bf16)
    end = jnp.concatenate([none, behind], axis=0).astype(bf16)
    end_late = jnp.concatenate([none, one, behind[0:1]], axis=0).astype(bf16)
    first = turned(top, conv[4]) + turned(top_late, conv[3])
    last = turned(end, conv[0]) + turned(end_late, conv[1])
    return jnp.concatenate([first, last], axis=0)


def slope_kernel(
    rows, total, own, near, far, weight, back, edges, cot, d_pooled, stem_part, gated, pooled, stem
):
    lanes = own.shape[1]
    width = cot.shape[1]
    padded = rows + 2 * LEAD
    codes = (own[...].astype(f32) + near[...].astype(f32) + far[...].astype(f32))[0:8]
    hot = one_hot(codes, lanes, LEAD - 2)[:, :padded]
    hot = jnp.concatenate([hot, hot, hot], axis=0)
    stem[...] = lax.dot_general(
        hot, weight[...], (((0,), (0,)), ((), ())), preferred_element_type=f32
    )
    mine = one_hot(codes, lanes, lanes - 2)
    first = lax.axis_index("context") * rows
    for edge in (0, LEAD + rows):
        act = 0.5 * (
            gelu_tanh(stem[edge : edge + LEAD, :width]) + gelu_tanh(stem[edge : edge + LEAD, width:])
        )
        act = act.astype(bf16).astype(f32)
        spot = first - LEAD + edge + lax.broadcasted_iota(jnp.int32, (LEAD, 1), 0)
        inside = (spot >= 0) & (spot < total)
        gated[edge : edge + LEAD, :] = jnp.where(inside, gelu_tanh(act), 0.0).astype(bf16)
    top, end = edges[0:8, :], edges[8:16, :]
    none = jnp.zeros((24, width), f32)
    step = 32
    for r in range(0, rows, step):
        even = stem[LEAD + r : LEAD + r + step, :width]
        odd = stem[LEAD + r : LEAD + r + step, width:]
        even, even_slope = gelu_both(even)
        odd, odd_slope = gelu_both(odd)
        low = (0.5 * (even + odd)).astype(bf16)
        pooled[r : r + step, :] = low
        gate, slope = gelu_both(low.astype(f32))
        gated[LEAD + r : LEAD + r + step, :] = gate.astype(bf16)
        rise = back[r : r + step, :]
        if r == 0:
            rise = rise + jnp.concatenate([top, none], axis=0)
        if r + step == rows:
            rise = rise + jnp.concatenate([none, end], axis=0)
        grad = cot[r : r + step, :].astype(f32) + rise * slope
        d_pooled[r : r + step, :] = grad.astype(bf16)
        half = 0.5 * grad
        stem[LEAD + r : LEAD + r + step, :width] = half * even_slope
        stem[LEAD + r : LEAD + r + step, width:] = half * odd_slope
    grads = jnp.dot(
        mine[:, :rows], stem[LEAD : LEAD + rows, :].astype(bf16), preferred_element_type=f32
    )
    even, odd = orders(stem_part.shape[0] // 4 - 1)
    for k in range(len(even) - 1):
        for a in range(4):
            p, q = 16 * a + even.index(k), 16 * a + odd.index(k)
            stem_part[4 * k + a : 4 * k + a + 1, :] = (
                grads[p : p + 1, :width] + grads[q : q + 1, width:]
            )
    stem_part[stem_part.shape[0] - 4 :, :] = jnp.zeros((4, width), f32)


def feature_kernel(rows, gated, pooled, conv, out):
    acc = pooled[...].astype(f32)
    for t in range(TAPS):
        start = LEAD - 2 + t
        acc = acc + jnp.dot(gated[start : start + rows, :], conv[t], preferred_element_type=f32)
    out[...] = acc.astype(bf16)


def put_pieces(pieces, out, room, sems):
    ctx, core, y = place_of()
    unit = room.shape[1]
    half = out.shape[1] // 2
    copies = []
    at = 0
    for piece, chain, flip, ids in pieces:
        tap, taps = ((0, FIRST), (FIRST, TAPS - FIRST))[chain]
        from_core = lax.rem(core + flip, 2)
        q = quarter_bit(ctx, from_core)
        for k, p in enumerate(ids):
            one, two = p % 2, p // 2
            dq = jnp.where(from_core == chain, one, two)
            dy = one + two - dq
            from_q, from_y = lax.rem(q + dq, 2), lax.rem(y + dy, 2)
            channel = from_y * half + (2 * from_core + from_q) * unit
            for t in range(taps):
                low = (k * taps + t) * unit
                room[at + t] = piece[low : low + unit, :].astype(f32)
            copy = pltpu.make_async_copy(
                room.at[pl.ds(at, taps)],
                out.at[pl.ds(tap, taps), pl.ds(pl.multiple_of(channel, 16), unit)],
                sems.at[len(copies)],
            )
            copy.start()
            copies.append(copy)
            at += taps
    return copies


def early_kernel(left, right, got_left, got_right, out, room, sems):
    pieces = [(left, 0, 0), (right, 1, 0), (got_left, 0, 1), (got_right, 1, 1)]
    for copy in put_pieces([(*piece, (0, 1)) for piece in pieces], out, room, sems):
        copy.wait()


def late_kernel(left, right, whole, out, room, sems):
    del whole
    for copy in put_pieces([(left, 0, 0, (2, 3)), (right, 1, 0, (2, 3))], out, room, sems):
        copy.wait()


def last_kernel(left, right, stem, whole, out, stem_out, room, sems):
    del whole
    copies = put_pieces([(left, 0, 1, (2, 3)), (right, 1, 1, (2, 3))], out, room, sems)
    mine = stem[...].astype(bf16).astype(f32)
    total = mine + right[right.shape[0] - stem.shape[0] :, :].astype(f32)
    for k in range(stem_out.shape[0]):
        stem_out[k] = total[4 * k : 4 * k + 4, :]
    for copy in copies:
        copy.wait()


def per_device(codes, variant_pos, variant_shift, stem_weight, conv_weight, cotangent):
    n_dp, n_ctx = lax.axis_size("dp"), lax.axis_size("context")
    devices = n_dp * n_ctx
    length = codes.shape[1]
    rows = length // 2
    taps, _, width = stem_weight.shape
    half = width // 2
    unit = half // 4
    total = rows * n_ctx
    lanes = -(-(rows + 256) // 128) * 128
    core = lax.axis_index("context") % 2
    cot = cotangent[0]
    x_bit, y_bit = 2, n_ctx
    z_bit = 4 if n_ctx % 8 == 0 else 2

    def swap(value, even_bit, odd_bit=None):
        odd_bit = even_bit if odd_bit is None else odd_bit
        pairs = [(i, i ^ (odd_bit if i & 1 else even_bit)) for i in range(devices)]
        return lax.ppermute(value, AXES, pairs)

    def call(kernel, out, operands, scratch=(), keep=(), **options):
        if keep:
            options["input_output_aliases"] = {
                len(operands) + k: len(out) + k for k in range(len(keep))
            }
            kernel = holding(kernel, len(operands), len(out), len(keep))
            operands = list(operands) + near_by(*keep)
            out = list(out) + [(value.shape, value.dtype) for value in keep]
        shapes = [jax.ShapeDtypeStruct(o[0], o[1]) for o in out]
        specs = [o[2] if len(o) > 2 else VMEM for o in out]
        options.setdefault("compiler_params", params())
        return pl.pallas_call(
            kernel,
            out_shape=shapes,
            in_specs=[spec for _, spec in operands],
            out_specs=specs,
            scratch_shapes=list(scratch),
            **options,
        )(*[value for value, _ in operands])

    def near_by(*values):
        return [(value, VMEM) for value in values]

    def far_off(*values):
        return [(pltpu.with_memory_space_constraint(value, pltpu.HBM), FAR) for value in values]

    outward = {}
    for d in range(n_dp):
        for c in range(n_ctx):
            other = c + 1 if c & 1 else c - 1
            if 0 <= other < n_ctx:
                outward[d * n_ctx + c] = d * n_ctx + other

    pair_cot = swap(cot, y_bit)
    dma = pltpu.SemaphoreType.DMA
    edge = ((16, lanes), bf16)
    own, near, far, weight, half_weight, cot_v, conv_v = call(
        functools.partial(first_kernel, rows, lanes),
        [
            edge,
            edge,
            edge,
            ((192, 2 * width), bf16),
            ((192, width), bf16),
            (cot.shape, bf16),
            (conv_weight.shape, bf16),
        ],
        far_off(codes, variant_pos, variant_shift, cot, stem_weight, conv_weight),
        [
            pltpu.VMEM((1, length), jnp.int32),
            pltpu.SMEM(variant_pos.shape, jnp.int32),
            pltpu.SMEM(variant_pos.shape, jnp.int32),
            pltpu.VMEM(stem_weight.shape, f32),
            dma((6,)),
        ],
        compiler_params=params(FIRST_LIMIT),
    )
    near = swap(near, 1)
    cost = pl.CostEstimate(
        flops=2 * TAPS * rows * width * width, bytes_accessed=4 << 20, transcendentals=0
    )
    padded = rows + 2 * LEAD
    (back,) = call(
        functools.partial(back_kernel, rows),
        [((rows, width), f32)],
        near_by(conv_v, cot_v),
        [pltpu.VMEM((padded, width), bf16)],
        cost_estimate=cost,
    )
    far = lax.ppermute(far, AXES, list(outward.items()))
    pair_codes = swap(after(own + near + far, back), y_bit)
    stem_half = pltpu.VMEM((width, rows + 128), f32)
    gates = ((TAPS * half, rows), bf16)
    part, edges, back = call(
        functools.partial(own_kernel, rows, total),
        [((TAPS * half, width), f32), ((16, width), f32)],
        near_by(own, near, far, half_weight, conv_v, cot_v),
        [stem_half, pltpu.VMEM(*gates)],
        keep=[back],
    )
    pair_gates, back = call(
        functools.partial(pair_kernel, rows, total),
        [gates],
        near_by(pair_codes, half_weight),
        [stem_half],
        keep=[back],
    )
    size = TAPS * half // 2
    sent, kept, back = call(
        sum_kernel,
        [((size, width), bf16), ((size, width), f32)],
        near_by(part, pair_gates, pair_cot),
        keep=[back],
    )
    got = swap(sent, 1)
    size //= 2
    sent, kept, back = call(
        split_kernel,
        [((size, width), bf16), ((size, width), f32)],
        near_by(kept, got),
        keep=[back],
    )
    got = swap(sent, x_bit, z_bit)
    d_pooled, stem_part, gated, pooled = call(
        functools.partial(slope_kernel, rows, total),
        [
            ((rows, width), bf16),
            ((4 * taps + 4, width), f32),
            ((padded, width), bf16),
            ((rows, width), bf16),
        ],
        near_by(after(own, sent), near, far, weight, back, edges, cot_v),
        [pltpu.VMEM((padded, 2 * width), f32)],
        cost_estimate=cost,
    )
    value = kept + got.astype(f32)

    cut = FIRST * unit
    rest = size - cut
    left = value[:cut]
    right = jnp.concatenate([value[cut:], stem_part], axis=0)
    bits = [1 << k for k in range(devices.bit_length() - 1)]
    even_rest = [b for b in bits if b not in (1, x_bit, y_bit)]
    odd_rest = [b for b in bits if b not in (1, z_bit, y_bit)]
    odd_rest = odd_rest[1:] + odd_rest[:1]
    for k, (b, odd_b) in enumerate(zip(even_rest, odd_rest)):
        left, right = rounded(left), rounded(right)
        if k == len(even_rest) - 1:
            pooled = after(pooled, right)
        left, right = [v + swap(v.astype(bf16), b, odd_b).astype(f32) for v in (left, right)]
    (features,) = call(
        functools.partial(feature_kernel, rows),
        [((rows, width), bf16)],
        near_by(gated, pooled, conv_v),
        cost_estimate=cost,
    )
    left, features = together(left, features)
    left = left.astype(bf16)
    stem_sum = right[rest:]
    right = right[:rest].astype(bf16)

    whole = ((TAPS, width, width), f32, FAR)

    def joined(pieces):
        return jnp.concatenate([pieces, stem_sum.astype(bf16)], axis=0)

    stem_sum = rounded(stem_sum)
    got_left, got_right = swap(left, x_bit, y_bit), swap(joined(right), y_bit, z_bit)
    left = jnp.concatenate([left, got_left], axis=0)
    stem_sum = stem_sum + got_right[rest:].astype(f32)
    right = jnp.concatenate([right, got_right[:rest]], axis=0)

    stem_sum = rounded(stem_sum)
    got_left, got_right = swap(left, y_bit, z_bit), swap(joined(right), x_bit, y_bit)
    (conv_grad,) = call(
        early_kernel,
        [whole],
        near_by(left, right, swap(left, 1), swap(right, 1)),
        [pltpu.VMEM((TAPS * 4, unit, width), f32), dma((8,))],
    )
    stem_sum = stem_sum + got_right[2 * rest :].astype(f32)
    left, right = got_left, got_right[: 2 * rest]
    left, conv_grad = together(left, conv_grad)
    got_left, got_right = swap(left, 1), swap(joined(right), 1)
    room = [pltpu.VMEM((TAPS * 2, unit, width), f32), dma((4,))]
    (conv_grad,) = call(
        late_kernel,
        [whole],
        near_by(left, right) + far_off(conv_grad),
        room,
        input_output_aliases={2: 0},
    )
    conv_grad, stem_grad = call(
        last_kernel,
        [whole, (stem_weight.shape, f32)],
        near_by(got_left, got_right, stem_sum) + far_off(conv_grad),
        room,
        input_output_aliases={3: 0},
    )
    return (features[None], d_pooled[None], conv_grad, stem_grad)


def solution(mesh):
    placed = (P("dp", "context"), P("dp", None), P("dp", None), P(), P(), P("dp", "context", None))
    return jax.shard_map(
        per_device,
        mesh=mesh,
        in_specs=placed,
        out_specs=(P("dp", "context", None), P("dp", "context", None), P(), P()),
        check_vma=False,
    )
```

```python
import functools
import math

import jax
import jax.numpy as jnp
from jax import lax
from jax.experimental import pallas as pl
from jax.experimental.pallas import tpu as pltpu
from jax.sharding import PartitionSpec as P

root_scale = math.sqrt(2.0 / math.pi)
cubic = 0.044715
AXES = ("dp", "context")
TAPS = 5
FIRST = 3
FIRST_LIMIT = 48
HALO = 6
LEAD = 16
VMEM = pl.BlockSpec(memory_space=pltpu.VMEM)
FAR = pl.BlockSpec(memory_space=pltpu.HBM)
bf16 = jnp.bfloat16
f32 = jnp.float32


def gelu_tanh(value):
    inner = jnp.tanh(value * (root_scale + (root_scale * cubic) * (value * value)))
    half = 0.5 * value
    return half + half * inner


def gelu_both(value):
    square = value * value
    inner = jnp.tanh(value * (root_scale + (root_scale * cubic) * square))
    rise = (1.0 - inner * inner) * (root_scale + (3.0 * root_scale * cubic) * square)
    half = 0.5 * value
    return half + half * inner, 0.5 + 0.5 * inner + half * rise


def rounded(value):
    return lax.reduce_precision(value, 8, 7)


def params(limit=24):
    return pltpu.CompilerParams(vmem_limit_bytes=limit * 1024 * 1024)


def together(*values):
    return lax.optimization_barrier(values)


def after(value, *others):
    return together(value, *others)[0]


def holding(kernel, operands, results, kept):
    def run(*refs):
        last = operands + kept + results
        kernel(*refs[:operands], *refs[operands + kept : last], *refs[last + kept :])

    return run


def first_kernel(
    rows,
    lanes,
    codes,
    positions,
    amounts,
    cot,
    own,
    near,
    far,
    base_v,
    pos_s,
    amt_s,
    top,
    bottom,
    sems,
):
    length = 2 * rows
    tiles = length // 128
    width = cot.shape[1]
    copies = [
        pltpu.make_async_copy(codes, base_v, sems.at[0]),
        pltpu.make_async_copy(positions, pos_s, sems.at[1]),
        pltpu.make_async_copy(amounts, amt_s, sems.at[2]),
        pltpu.make_async_copy(cot.at[pl.ds(0, 16)], top, sems.at[3]),
        pltpu.make_async_copy(cot.at[pl.ds(rows - 16, 16)], bottom, sems.at[4]),
    ]
    for copy in copies:
        copy.start()
    ctx = lax.axis_index("context")
    core = lax.rem(ctx, 2)
    for copy in copies:
        copy.wait()
    x = jnp.concatenate([base_v[:, 128 * q : 128 * q + 128] for q in range(tiles)], axis=0)
    spot = (
        ctx * length
        + 128 * lax.broadcasted_iota(jnp.int32, x.shape, 0)
        + lax.broadcasted_iota(jnp.int32, x.shape, 1)
    )
    sums = [x] + [jnp.zeros_like(x)] * 3
    for v in range(positions.shape[1]):
        sums[v % 4] = sums[v % 4] + jnp.where(spot == pos_s[0, v], amt_s[0, v], 0)
    x = (sums[0] + sums[1]) + (sums[2] + sums[3])
    x = ((x & 3) + 1).astype(f32).astype(bf16)
    source = lax.broadcasted_iota(jnp.int32, (128, 128), 0)
    target = lax.broadcasted_iota(jnp.int32, (128, 128), 1)

    def picked(parity):
        left = (source == 2 * target + parity).astype(f32).astype(bf16)
        right = (source == 2 * (target - 64) + parity).astype(f32).astype(bf16)
        low = jnp.dot(x, left, preferred_element_type=f32)
        high = jnp.dot(x, right, preferred_element_type=f32)
        parts = [low[2 * q : 2 * q + 1] + high[2 * q + 1 : 2 * q + 2] for q in range(tiles // 2)]
        return jnp.concatenate(parts + [jnp.zeros((1, lanes - rows), f32)], axis=1)

    both = jnp.concatenate([picked(0), picked(1), jnp.zeros((6, lanes), f32)], axis=0)
    lane = lax.broadcasted_iota(jnp.int32, both.shape, 1)
    shifted = pltpu.roll(both, HALO, 1)
    last = jnp.where(lane < HALO, pltpu.roll(both, lanes - (rows - HALO), 1), 0.0)
    ahead = (lane >= rows + HALO) & (lane < rows + 2 * HALO)
    first = jnp.where(ahead, pltpu.roll(both, rows + HALO, 1), 0.0)
    blank = jnp.zeros((8, lanes), f32)
    pad = jnp.zeros((2, lanes - width), f32)

    def message(edge, grads):
        grads = jnp.concatenate([grads, pad], axis=1)
        return jnp.concatenate([edge, grads, jnp.zeros((6, lanes), f32)], axis=0)

    head = message(first, top[...].astype(f32)[0:2])
    tail = message(last, bottom[...].astype(f32)[14:16])
    own[...] = jnp.concatenate([shifted, blank], axis=0).astype(bf16)
    near[...] = jnp.where(core == 0, tail, head).astype(bf16)
    far[...] = jnp.where(core == 0, head, tail).astype(bf16)


def second_kernel(
    cot, stem_weight, conv, near, weight, half_weight, cot_out, conv_out, weight_v, sems
):
    del near
    copies = [
        pltpu.make_async_copy(stem_weight, weight_v, sems.at[0]),
        pltpu.make_async_copy(cot, cot_out, sems.at[1]),
        pltpu.make_async_copy(conv, conv_out, sems.at[2]),
    ]
    for copy in copies:
        copy.start()
    copies[0].wait()
    stem_terms(weight_v, weight, half_weight)
    for copy in copies[1:]:
        copy.wait()


def stem_terms(weight, out, half_out):
    width = weight.shape[2]
    zero = jnp.zeros((1, width), f32)
    even, odd = orders(weight.shape[0])

    def rows(order):
        return jnp.concatenate(
            [
                zero if k is None else weight[k, a : a + 1, :]
                for a in range(4)
                for k in order
            ],
            axis=0,
        )

    def terms(full):
        high = full.astype(bf16)
        left = full - high.astype(f32)
        middle = left.astype(bf16)
        low = (left - middle.astype(f32)).astype(bf16)
        return jnp.concatenate([high, middle, low], axis=0)

    evens, odds = rows(even), rows(odd)
    half = width // 2
    upper = lax.rem(lax.axis_index("dp"), 2) == 1
    out[...] = terms(jnp.concatenate([evens, odds], axis=1))
    mine = [jnp.where(upper, v[:, half:], v[:, :half]) for v in (evens, odds)]
    half_out[...] = terms(jnp.concatenate(mine, axis=1))


def orders(taps):
    even = [None] + list(range(taps - 2, 0, -2)) + list(range(taps - 1, -1, -2))
    odd = list(range(taps - 1, -1, -2)) + list(range(taps - 2, 0, -2)) + [None]
    return even, odd


def one_hot(codes, lanes, shift):
    even = jnp.broadcast_to(codes[0:1], (8, lanes))
    odd = jnp.broadcast_to(codes[1:2], (8, lanes))
    even = pltpu.roll(even, (2 * lanes - 8 + shift) % lanes, 1, stride=1, stride_axis=0)
    odd = pltpu.roll(odd, (2 * lanes - 7 + shift) % lanes, 1, stride=1, stride_axis=0)
    near = jnp.concatenate([even, odd], axis=0)
    return jnp.concatenate([(near == a + 1.0).astype(f32) for a in range(4)], axis=0).astype(bf16)


def shifted_gates(codes, first, total, weight, rows, stem, gated):
    used = rows + 128
    half = weight.shape[1] // 2
    quarter = half // 4
    hot = one_hot(codes, codes.shape[1], 0)[:, :used]
    hot = jnp.concatenate([hot, hot, hot], axis=0)
    stem[...] = lax.dot_general(
        weight[...], hot, (((0,), (0,)), ((), ())), preferred_element_type=f32
    )
    spot = first - 2 + lax.broadcasted_iota(jnp.int32, (1, used), 1)
    inside = (spot >= 0) & (spot < total)
    step = 16
    for c in range(0, half, step):
        even = gelu_tanh(stem[c : c + step, :])
        odd = gelu_tanh(stem[half + c : half + c + step, :])
        pooled = (0.5 * (even + odd)).astype(bf16).astype(f32)
        value = jnp.where(inside, gelu_tanh(pooled), 0.0)
        for t in range(TAPS):
            moved = value if t == 0 else pltpu.roll(value, used - t, 1)
            at = (c // quarter * TAPS + t) * quarter + c % quarter
            gated[at : at + step, :] = moved[:, :rows].astype(bf16)


def own_kernel(rows, total, own, near, far, weight, conv, cot, out, edges, stem, gated):
    first = lax.axis_index("context") * rows
    codes = (own[...].astype(f32) + near[...].astype(f32) + far[...].astype(f32))[0:8]
    shifted_gates(codes, first, total, weight, rows, stem, gated)
    edges[...] = edge_terms(near, far, conv)
    out[...] = jnp.dot(gated[...], cot[...], preferred_element_type=f32)


def pair_kernel(rows, total, codes, weight, gated, stem):
    first = lax.axis_index("context") * rows
    shifted_gates(codes[...].astype(f32)[0:8], first, total, weight, rows, stem, gated)


def sum_kernel(part, gated, cot, sent, kept):
    core = lax.rem(lax.axis_index("context"), 2)
    size = sent.shape[0]
    for which, out in ((1 - core, sent), (core, kept)):
        span = pl.ds(pl.multiple_of(which * size, 16), size)
        value = part[span, :] + jnp.dot(gated[span, :], cot[...], preferred_element_type=f32)
        out[...] = value.astype(out.dtype)


def place_of():
    ctx = lax.axis_index("context")
    return ctx, lax.rem(ctx, 2), lax.rem(lax.axis_index("dp"), 2)


def quarter_bit(ctx, core):
    far = 4 if lax.axis_size("context") % 8 == 0 else 2
    return jnp.where(core == 0, lax.rem(ctx // 2, 2), lax.rem(ctx // far, 2))


def split_kernel(value, got, sent, kept):
    x = quarter_bit(*place_of()[:2])
    size = sent.shape[0]
    for which, out in ((1 - x, sent), (x, kept)):
        span = pl.ds(pl.multiple_of(which * size, 16), size)
        out[...] = (value[span, :] + got[span, :].astype(f32)).astype(out.dtype)


def back_kernel(rows, conv, cot, back, ext):
    width = cot.shape[1]
    blank = jnp.zeros((LEAD, width), bf16)
    ext[0:LEAD, :] = blank
    ext[LEAD : LEAD + rows, :] = cot[...]
    ext[LEAD + rows :, :] = blank
    for t in range(TAPS):
        start = LEAD + 2 - t
        term = turned(ext[start : start + rows, :], conv[t])
        back[...] = term if t == 0 else back[...] + term


def turned(left, right):
    return lax.dot_general(left, right, (((1,), (1,)), ((), ())), preferred_element_type=f32)


def edge_terms(near, far, conv):
    width = conv.shape[1]
    core = lax.rem(lax.axis_index("context"), 2)
    near_v, far_v = near[...].astype(f32), far[...].astype(f32)
    before = jnp.where(core == 0, far_v, near_v)[8:10, :width]
    behind = jnp.where(core == 0, near_v, far_v)[8:10, :width]
    none = jnp.zeros((6, width), f32)
    one = jnp.zeros((1, width), f32)
    top = jnp.concatenate([before, none], axis=0).astype(bf16)
    top_late = jnp.concatenate([before[1:2], one, none], axis=0).astype(bf16)
    end = jnp.concatenate([none, behind], axis=0).astype(bf16)
    end_late = jnp.concatenate([none, one, behind[0:1]], axis=0).astype(bf16)
    first = turned(top, conv[4]) + turned(top_late, conv[3])
    last = turned(end, conv[0]) + turned(end_late, conv[1])
    return jnp.concatenate([first, last], axis=0)


def slope_kernel(
    rows, total, own, near, far, weight, back, edges, cot, d_pooled, stem_part, gated, pooled, stem
):
    lanes = own.shape[1]
    width = cot.shape[1]
    padded = rows + 2 * LEAD
    codes = (own[...].astype(f32) + near[...].astype(f32) + far[...].astype(f32))[0:8]
    hot = one_hot(codes, lanes, LEAD - 2)[:, :padded]
    hot = jnp.concatenate([hot, hot, hot], axis=0)
    stem[...] = lax.dot_general(
        hot, weight[...], (((0,), (0,)), ((), ())), preferred_element_type=f32
    )
    mine = one_hot(codes, lanes, lanes - 2)
    first = lax.axis_index("context") * rows
    for edge in (0, LEAD + rows):
        act = 0.5 * (
            gelu_tanh(stem[edge : edge + LEAD, :width]) + gelu_tanh(stem[edge : edge + LEAD, width:])
        )
        act = act.astype(bf16).astype(f32)
        spot = first - LEAD + edge + lax.broadcasted_iota(jnp.int32, (LEAD, 1), 0)
        inside = (spot >= 0) & (spot < total)
        gated[edge : edge + LEAD, :] = jnp.where(inside, gelu_tanh(act), 0.0).astype(bf16)
    top, end = edges[0:8, :], edges[8:16, :]
    none = jnp.zeros((24, width), f32)
    step = 32
    for r in range(0, rows, step):
        even = stem[LEAD + r : LEAD + r + step, :width]
        odd = stem[LEAD + r : LEAD + r + step, width:]
        even, even_slope = gelu_both(even)
        odd, odd_slope = gelu_both(odd)
        low = (0.5 * (even + odd)).astype(bf16)
        pooled[r : r + step, :] = low
        gate, slope = gelu_both(low.astype(f32))
        gated[LEAD + r : LEAD + r + step, :] = gate.astype(bf16)
        rise = back[r : r + step, :]
        if r == 0:
            rise = rise + jnp.concatenate([top, none], axis=0)
        if r + step == rows:
            rise = rise + jnp.concatenate([none, end], axis=0)
        grad = cot[r : r + step, :].astype(f32) + rise * slope
        d_pooled[r : r + step, :] = grad.astype(bf16)
        half = 0.5 * grad
        stem[LEAD + r : LEAD + r + step, :width] = half * even_slope
        stem[LEAD + r : LEAD + r + step, width:] = half * odd_slope
    grads = jnp.dot(
        mine[:, :rows], stem[LEAD : LEAD + rows, :].astype(bf16), preferred_element_type=f32
    )
    even, odd = orders(stem_part.shape[0] // 4 - 1)
    for k in range(len(even) - 1):
        for a in range(4):
            p, q = 16 * a + even.index(k), 16 * a + odd.index(k)
            stem_part[4 * k + a : 4 * k + a + 1, :] = (
                grads[p : p + 1, :width] + grads[q : q + 1, width:]
            )
    stem_part[stem_part.shape[0] - 4 :, :] = jnp.zeros((4, width), f32)


def feature_kernel(rows, gated, pooled, conv, out):
    acc = pooled[...].astype(f32)
    for t in range(TAPS):
        start = LEAD - 2 + t
        acc = acc + jnp.dot(gated[start : start + rows, :], conv[t], preferred_element_type=f32)
    out[...] = acc.astype(bf16)


def put_pieces(pieces, out, room, sems):
    ctx, core, y = place_of()
    unit = room.shape[1]
    half = out.shape[1] // 2
    copies = []
    at = 0
    for piece, chain, flip, ids in pieces:
        tap, taps = ((0, FIRST), (FIRST, TAPS - FIRST))[chain]
        from_core = lax.rem(core + flip, 2)
        q = quarter_bit(ctx, from_core)
        for k, p in enumerate(ids):
            from_q, from_y = lax.rem(q + p // 2, 2), lax.rem(y + p % 2, 2)
            channel = from_y * half + (2 * from_core + from_q) * unit
            for t in range(taps):
                low = (k * taps + t) * unit
                room[at + t] = piece[low : low + unit, :].astype(f32)
            copy = pltpu.make_async_copy(
                room.at[pl.ds(at, taps)],
                out.at[pl.ds(tap, taps), pl.ds(pl.multiple_of(channel, 16), unit)],
                sems.at[len(copies)],
            )
            copy.start()
            copies.append(copy)
            at += taps
    return copies


def early_kernel(left, right, got_left, got_right, out, room, sems):
    pieces = [(left, 0, 0), (right, 1, 0), (got_left, 0, 1), (got_right, 1, 1)]
    for copy in put_pieces([(*piece, (0, 1)) for piece in pieces], out, room, sems):
        copy.wait()


def late_kernel(left, right, got_left, whole, out, room, sems):
    del whole
    pieces = [(left, 0, 0, (2, 3)), (right, 1, 0, (2, 3)), (got_left, 0, 1, (2, 3))]
    for copy in put_pieces(pieces, out, room, sems):
        copy.wait()


def last_kernel(right, stem, whole, out, stem_out, room, sems, stem_v, stem_sem):
    del whole
    mine = stem[...].astype(bf16).astype(f32)
    total = mine + right[right.shape[0] - stem.shape[0] :, :].astype(f32)
    for k in range(stem_out.shape[0]):
        stem_v[k] = total[4 * k : 4 * k + 4, :]
    copy = pltpu.make_async_copy(stem_v, stem_out, stem_sem)
    copy.start()
    copies = put_pieces([(right, 1, 1, (2, 3))], out, room, sems)
    for done in [*copies, copy]:
        done.wait()


def per_device(codes, variant_pos, variant_shift, stem_weight, conv_weight, cotangent):
    n_dp, n_ctx = lax.axis_size("dp"), lax.axis_size("context")
    devices = n_dp * n_ctx
    length = codes.shape[1]
    rows = length // 2
    taps, _, width = stem_weight.shape
    half = width // 2
    unit = half // 4
    total = rows * n_ctx
    lanes = -(-(rows + 256) // 128) * 128
    core = lax.axis_index("context") % 2
    cot = cotangent[0]
    x_bit, y_bit = 2, n_ctx
    z_bit = 4 if n_ctx % 8 == 0 else 2

    def swap(value, even_bit, odd_bit=None):
        odd_bit = even_bit if odd_bit is None else odd_bit
        pairs = [(i, i ^ (odd_bit if i & 1 else even_bit)) for i in range(devices)]
        return lax.ppermute(value, AXES, pairs)

    def call(kernel, out, operands, scratch=(), keep=(), **options):
        if keep:
            options["input_output_aliases"] = {
                len(operands) + k: len(out) + k for k in range(len(keep))
            }
            kernel = holding(kernel, len(operands), len(out), len(keep))
            operands = list(operands) + near_by(*keep)
            out = list(out) + [(value.shape, value.dtype) for value in keep]
        shapes = [jax.ShapeDtypeStruct(o[0], o[1]) for o in out]
        specs = [o[2] if len(o) > 2 else VMEM for o in out]
        options.setdefault("compiler_params", params())
        return pl.pallas_call(
            kernel,
            out_shape=shapes,
            in_specs=[spec for _, spec in operands],
            out_specs=specs,
            scratch_shapes=list(scratch),
            **options,
        )(*[value for value, _ in operands])

    def near_by(*values):
        return [(value, VMEM) for value in values]

    def far_off(*values):
        return [(pltpu.with_memory_space_constraint(value, pltpu.HBM), FAR) for value in values]

    outward = {}
    for d in range(n_dp):
        for c in range(n_ctx):
            other = c + 1 if c & 1 else c - 1
            if 0 <= other < n_ctx:
                outward[d * n_ctx + c] = d * n_ctx + other

    pair_cot = swap(cot, y_bit)
    dma = pltpu.SemaphoreType.DMA
    edge = ((16, lanes), bf16)
    own, near, far = call(
        functools.partial(first_kernel, rows, lanes),
        [edge, edge, edge],
        far_off(codes, variant_pos, variant_shift, cot),
        [
            pltpu.VMEM((1, length), jnp.int32),
            pltpu.SMEM(variant_pos.shape, jnp.int32),
            pltpu.SMEM(variant_pos.shape, jnp.int32),
            pltpu.VMEM((16, width), bf16),
            pltpu.VMEM((16, width), bf16),
            dma((5,)),
        ],
        compiler_params=params(FIRST_LIMIT),
    )
    weight, half_weight, cot_v, conv_v = call(
        second_kernel,
        [
            ((192, 2 * width), bf16),
            ((192, width), bf16),
            (cot.shape, bf16),
            (conv_weight.shape, bf16),
        ],
        far_off(cot, stem_weight, conv_weight) + near_by(near),
        [pltpu.VMEM(stem_weight.shape, f32), dma((3,))],
    )
    near = swap(near, 1)
    cost = pl.CostEstimate(
        flops=2 * TAPS * rows * width * width, bytes_accessed=4 << 20, transcendentals=0
    )
    padded = rows + 2 * LEAD
    (back,) = call(
        functools.partial(back_kernel, rows),
        [((rows, width), f32)],
        near_by(conv_v, cot_v),
        [pltpu.VMEM((padded, width), bf16)],
        cost_estimate=cost,
    )
    far = lax.ppermute(far, AXES, list(outward.items()))
    pair_codes = swap(own + near + far, y_bit)
    stem_half = pltpu.VMEM((width, rows + 128), f32)
    gates = ((TAPS * half, rows), bf16)
    part, edges, back = call(
        functools.partial(own_kernel, rows, total),
        [((TAPS * half, width), f32), ((16, width), f32)],
        near_by(own, near, far, half_weight, conv_v, cot_v),
        [stem_half, pltpu.VMEM(*gates)],
        keep=[back],
    )
    pair_gates, back = call(
        functools.partial(pair_kernel, rows, total),
        [gates],
        near_by(pair_codes, half_weight),
        [stem_half],
        keep=[back],
    )
    size = TAPS * half // 2
    sent, kept, back = call(
        sum_kernel,
        [((size, width), bf16), ((size, width), f32)],
        near_by(part, pair_gates, pair_cot),
        keep=[back],
    )
    got = swap(sent, 1)
    size //= 2
    sent, kept, back = call(
        split_kernel,
        [((size, width), bf16), ((size, width), f32)],
        near_by(kept, got),
        keep=[back],
    )
    got = swap(sent, x_bit, z_bit)
    d_pooled, stem_part, gated, pooled = call(
        functools.partial(slope_kernel, rows, total),
        [
            ((rows, width), bf16),
            ((4 * taps + 4, width), f32),
            ((padded, width), bf16),
            ((rows, width), bf16),
        ],
        near_by(after(own, sent), near, far, weight, back, edges, cot_v),
        [pltpu.VMEM((padded, 2 * width), f32)],
        cost_estimate=cost,
    )
    value = kept + got.astype(f32)

    cut = FIRST * unit
    rest = size - cut
    left = value[:cut]
    right = jnp.concatenate([value[cut:], stem_part], axis=0)
    bits = [1 << k for k in range(devices.bit_length() - 1)]
    even_rest = [b for b in bits if b not in (1, x_bit, y_bit)]
    odd_rest = [b for b in bits if b not in (1, z_bit, y_bit)]
    odd_rest = odd_rest[1:] + odd_rest[:1]
    for k, (b, odd_b) in enumerate(zip(even_rest, odd_rest)):
        left, right = rounded(left), rounded(right)
        if k == 0:
            pooled = after(pooled, right.astype(bf16))
        left, right = [v + swap(v.astype(bf16), b, odd_b).astype(f32) for v in (left, right)]
    (features,) = call(
        functools.partial(feature_kernel, rows),
        [((rows, width), bf16)],
        near_by(gated, pooled, conv_v),
        cost_estimate=cost,
    )
    left, features = together(left, features)
    left = left.astype(bf16)
    stem_sum = right[rest:]
    right = right[:rest].astype(bf16)

    whole = ((TAPS, width, width), f32, FAR)

    def joined(pieces):
        return jnp.concatenate([pieces, stem_sum.astype(bf16)], axis=0)

    stem_sum = rounded(stem_sum)
    got_left, got_right = swap(left, y_bit), swap(joined(right), y_bit)
    left = jnp.concatenate([left, got_left], axis=0)
    stem_sum = stem_sum + got_right[rest:].astype(f32)
    right = jnp.concatenate([right, got_right[:rest]], axis=0)

    stem_sum = rounded(stem_sum)
    got_left, got_right = swap(left, x_bit, z_bit), swap(joined(right), x_bit, z_bit)
    (conv_grad,) = call(
        early_kernel,
        [whole],
        near_by(left, right, swap(left, 1), swap(right, 1)),
        [pltpu.VMEM((TAPS * 4, unit, width), f32), dma((8,))],
    )
    stem_sum = stem_sum + got_right[2 * rest :].astype(f32)
    left, right = got_left, got_right[: 2 * rest]
    left, conv_grad = together(left, conv_grad)
    got_left, got_right = swap(left, 1), swap(joined(right), 1)
    (conv_grad,) = call(
        late_kernel,
        [whole],
        near_by(left, right, got_left) + far_off(conv_grad),
        [pltpu.VMEM((2 * (TAPS + FIRST), unit, width), f32), dma((6,))],
        input_output_aliases={3: 0},
    )
    conv_grad, stem_grad = call(
        last_kernel,
        [whole, (stem_weight.shape, f32, FAR)],
        near_by(got_right, stem_sum) + far_off(conv_grad),
        [
            pltpu.VMEM((2 * (TAPS - FIRST), unit, width), f32),
            dma((2,)),
            pltpu.VMEM(stem_weight.shape, f32),
            dma,
        ],
        input_output_aliases={2: 0},
    )
    return (features[None], d_pooled[None], conv_grad, stem_grad)


def solution(mesh):
    placed = (P("dp", "context"), P("dp", None), P("dp", None), P(), P(), P("dp", "context", None))
    return jax.shard_map(
        per_device,
        mesh=mesh,
        in_specs=placed,
        out_specs=(P("dp", "context", None), P("dp", "context", None), P(), P()),
        check_vma=False,
    )
```

```python
import functools
import math

import jax
import jax.numpy as jnp
from jax import lax
from jax.experimental import pallas as pl
from jax.experimental.pallas import tpu as pltpu
from jax.sharding import PartitionSpec as P

root_scale = math.sqrt(2.0 / math.pi)
cubic = 0.044715
AXES = ("dp", "context")
TAPS = 5
FIRST = 3
FIRST_LIMIT = 48
HALO = 6
LEAD = 16
VMEM = pl.BlockSpec(memory_space=pltpu.VMEM)
FAR = pl.BlockSpec(memory_space=pltpu.HBM)
bf16 = jnp.bfloat16
f32 = jnp.float32


def gelu_tanh(value):
    inner = jnp.tanh(value * (root_scale + (root_scale * cubic) * (value * value)))
    half = 0.5 * value
    return half + half * inner


def gelu_both(value):
    square = value * value
    inner = jnp.tanh(value * (root_scale + (root_scale * cubic) * square))
    rise = (1.0 - inner * inner) * (root_scale + (3.0 * root_scale * cubic) * square)
    half = 0.5 * value
    return half + half * inner, 0.5 + 0.5 * inner + half * rise


def rounded(value):
    return lax.reduce_precision(value, 8, 7)


def params(limit=24):
    return pltpu.CompilerParams(vmem_limit_bytes=limit * 1024 * 1024)


def together(*values):
    return lax.optimization_barrier(values)


def after(value, *others):
    return together(value, *others)[0]


def holding(kernel, operands, results, kept):
    def run(*refs):
        last = operands + kept + results
        kernel(*refs[:operands], *refs[operands + kept : last], *refs[last + kept :])

    return run


def first_kernel(
    rows,
    lanes,
    codes,
    positions,
    amounts,
    cot,
    own,
    near,
    far,
    base_v,
    pos_s,
    amt_s,
    top,
    bottom,
    sems,
):
    length = 2 * rows
    tiles = length // 128
    width = cot.shape[1]
    copies = [
        pltpu.make_async_copy(codes, base_v, sems.at[0]),
        pltpu.make_async_copy(positions, pos_s, sems.at[1]),
        pltpu.make_async_copy(amounts, amt_s, sems.at[2]),
        pltpu.make_async_copy(cot.at[pl.ds(0, 16)], top, sems.at[3]),
        pltpu.make_async_copy(cot.at[pl.ds(rows - 16, 16)], bottom, sems.at[4]),
    ]
    for copy in copies:
        copy.start()
    ctx = lax.axis_index("context")
    core = lax.rem(ctx, 2)
    for copy in copies:
        copy.wait()
    x = jnp.concatenate([base_v[:, 128 * q : 128 * q + 128] for q in range(tiles)], axis=0)
    spot = (
        ctx * length
        + 128 * lax.broadcasted_iota(jnp.int32, x.shape, 0)
        + lax.broadcasted_iota(jnp.int32, x.shape, 1)
    )
    sums = [x] + [jnp.zeros_like(x)] * 3
    for v in range(positions.shape[1]):
        sums[v % 4] = sums[v % 4] + jnp.where(spot == pos_s[0, v], amt_s[0, v], 0)
    x = (sums[0] + sums[1]) + (sums[2] + sums[3])
    x = ((x & 3) + 1).astype(f32).astype(bf16)
    source = lax.broadcasted_iota(jnp.int32, (128, 128), 0)
    target = lax.broadcasted_iota(jnp.int32, (128, 128), 1)

    def picked(parity):
        left = (source == 2 * target + parity).astype(f32).astype(bf16)
        right = (source == 2 * (target - 64) + parity).astype(f32).astype(bf16)
        low = jnp.dot(x, left, preferred_element_type=f32)
        high = jnp.dot(x, right, preferred_element_type=f32)
        parts = [low[2 * q : 2 * q + 1] + high[2 * q + 1 : 2 * q + 2] for q in range(tiles // 2)]
        return jnp.concatenate(parts + [jnp.zeros((1, lanes - rows), f32)], axis=1)

    both = jnp.concatenate([picked(0), picked(1), jnp.zeros((6, lanes), f32)], axis=0)
    lane = lax.broadcasted_iota(jnp.int32, both.shape, 1)
    shifted = pltpu.roll(both, HALO, 1)
    last = jnp.where(lane < HALO, pltpu.roll(both, lanes - (rows - HALO), 1), 0.0)
    ahead = (lane >= rows + HALO) & (lane < rows + 2 * HALO)
    first = jnp.where(ahead, pltpu.roll(both, rows + HALO, 1), 0.0)
    blank = jnp.zeros((8, lanes), f32)
    pad = jnp.zeros((2, lanes - width), f32)

    def message(edge, grads):
        grads = jnp.concatenate([grads, pad], axis=1)
        return jnp.concatenate([edge, grads, jnp.zeros((6, lanes), f32)], axis=0)

    head = message(first, top[...].astype(f32)[0:2])
    tail = message(last, bottom[...].astype(f32)[14:16])
    own[...] = jnp.concatenate([shifted, blank], axis=0).astype(bf16)
    near[...] = jnp.where(core == 0, tail, head).astype(bf16)
    far[...] = jnp.where(core == 0, head, tail).astype(bf16)


def second_kernel(
    cot, stem_weight, conv, near, weight, half_weight, cot_out, conv_out, weight_v, sems
):
    del near
    copies = [
        pltpu.make_async_copy(stem_weight, weight_v, sems.at[0]),
        pltpu.make_async_copy(cot, cot_out, sems.at[1]),
        pltpu.make_async_copy(conv, conv_out, sems.at[2]),
    ]
    for copy in copies:
        copy.start()
    copies[0].wait()
    stem_terms(weight_v, weight, half_weight)
    for copy in copies[1:]:
        copy.wait()


def stem_terms(weight, out, half_out):
    width = weight.shape[2]
    zero = jnp.zeros((1, width), f32)
    even, odd = orders(weight.shape[0])

    def rows(order):
        return jnp.concatenate(
            [
                zero if k is None else weight[k, a : a + 1, :]
                for a in range(4)
                for k in order
            ],
            axis=0,
        )

    def terms(full):
        high = full.astype(bf16)
        left = full - high.astype(f32)
        middle = left.astype(bf16)
        low = (left - middle.astype(f32)).astype(bf16)
        return jnp.concatenate([high, middle, low], axis=0)

    evens, odds = rows(even), rows(odd)
    half = width // 2
    upper = lax.rem(lax.axis_index("dp"), 2) == 1
    out[...] = terms(jnp.concatenate([evens, odds], axis=1))
    mine = [jnp.where(upper, v[:, half:], v[:, :half]) for v in (evens, odds)]
    half_out[...] = terms(jnp.concatenate(mine, axis=1))


def orders(taps):
    even = [None] + list(range(taps - 2, 0, -2)) + list(range(taps - 1, -1, -2))
    odd = list(range(taps - 1, -1, -2)) + list(range(taps - 2, 0, -2)) + [None]
    return even, odd


def one_hot(codes, lanes, shift):
    even = jnp.broadcast_to(codes[0:1], (8, lanes))
    odd = jnp.broadcast_to(codes[1:2], (8, lanes))
    even = pltpu.roll(even, (2 * lanes - 8 + shift) % lanes, 1, stride=1, stride_axis=0)
    odd = pltpu.roll(odd, (2 * lanes - 7 + shift) % lanes, 1, stride=1, stride_axis=0)
    near = jnp.concatenate([even, odd], axis=0)
    return jnp.concatenate([(near == a + 1.0).astype(f32) for a in range(4)], axis=0).astype(bf16)


def shifted_gates(codes, first, total, weight, rows, stem, gated):
    used = rows + 128
    half = weight.shape[1] // 2
    quarter = half // 4
    hot = one_hot(codes, codes.shape[1], 0)[:, :used]
    hot = jnp.concatenate([hot, hot, hot], axis=0)
    stem[...] = lax.dot_general(
        weight[...], hot, (((0,), (0,)), ((), ())), preferred_element_type=f32
    )
    spot = first - 2 + lax.broadcasted_iota(jnp.int32, (1, used), 1)
    inside = (spot >= 0) & (spot < total)
    step = 16
    for c in range(0, half, step):
        even = gelu_tanh(stem[c : c + step, :])
        odd = gelu_tanh(stem[half + c : half + c + step, :])
        pooled = (0.5 * (even + odd)).astype(bf16).astype(f32)
        value = jnp.where(inside, gelu_tanh(pooled), 0.0)
        for t in range(TAPS):
            moved = value if t == 0 else pltpu.roll(value, used - t, 1)
            at = (c // quarter * TAPS + t) * quarter + c % quarter
            gated[at : at + step, :] = moved[:, :rows].astype(bf16)


def own_kernel(rows, total, own, near, far, weight, conv, cot, out, edges, stem, gated):
    first = lax.axis_index("context") * rows
    codes = (own[...].astype(f32) + near[...].astype(f32) + far[...].astype(f32))[0:8]
    shifted_gates(codes, first, total, weight, rows, stem, gated)
    edges[...] = edge_terms(near, far, conv)
    out[...] = jnp.dot(gated[...], cot[...], preferred_element_type=f32)


def pair_kernel(rows, total, codes, weight, gated, stem):
    first = lax.axis_index("context") * rows
    shifted_gates(codes[...].astype(f32)[0:8], first, total, weight, rows, stem, gated)


def sum_kernel(part, gated, cot, sent, kept):
    core = lax.rem(lax.axis_index("context"), 2)
    size = sent.shape[0]
    for which, out in ((1 - core, sent), (core, kept)):
        span = pl.ds(pl.multiple_of(which * size, 16), size)
        value = part[span, :] + jnp.dot(gated[span, :], cot[...], preferred_element_type=f32)
        out[...] = value.astype(out.dtype)


def place_of():
    ctx = lax.axis_index("context")
    return ctx, lax.rem(ctx, 2), lax.rem(lax.axis_index("dp"), 2)


def quarter_bit(ctx, core):
    far = 4 if lax.axis_size("context") % 8 == 0 else 2
    return jnp.where(core == 0, lax.rem(ctx // far, 2), lax.rem(ctx // 2, 2))


def split_kernel(value, got, sent, kept):
    x = quarter_bit(*place_of()[:2])
    size = sent.shape[0]
    for which, out in ((1 - x, sent), (x, kept)):
        span = pl.ds(pl.multiple_of(which * size, 16), size)
        out[...] = (value[span, :] + got[span, :].astype(f32)).astype(out.dtype)


def back_kernel(rows, conv, cot, back, ext):
    width = cot.shape[1]
    blank = jnp.zeros((LEAD, width), bf16)
    ext[0:LEAD, :] = blank
    ext[LEAD : LEAD + rows, :] = cot[...]
    ext[LEAD + rows :, :] = blank
    for t in range(TAPS):
        start = LEAD + 2 - t
        term = turned(ext[start : start + rows, :], conv[t])
        back[...] = term if t == 0 else back[...] + term


def turned(left, right):
    return lax.dot_general(left, right, (((1,), (1,)), ((), ())), preferred_element_type=f32)


def edge_terms(near, far, conv):
    width = conv.shape[1]
    core = lax.rem(lax.axis_index("context"), 2)
    near_v, far_v = near[...].astype(f32), far[...].astype(f32)
    before = jnp.where(core == 0, far_v, near_v)[8:10, :width]
    behind = jnp.where(core == 0, near_v, far_v)[8:10, :width]
    none = jnp.zeros((6, width), f32)
    one = jnp.zeros((1, width), f32)
    top = jnp.concatenate([before, none], axis=0).astype(bf16)
    top_late = jnp.concatenate([before[1:2], one, none], axis=0).astype(bf16)
    end = jnp.concatenate([none, behind], axis=0).astype(bf16)
    end_late = jnp.concatenate([none, one, behind[0:1]], axis=0).astype(bf16)
    first = turned(top, conv[4]) + turned(top_late, conv[3])
    last = turned(end, conv[0]) + turned(end_late, conv[1])
    return jnp.concatenate([first, last], axis=0)


def slope_kernel(
    rows, total, own, near, far, weight, back, edges, cot, d_pooled, stem_part, gated, pooled, stem
):
    lanes = own.shape[1]
    width = cot.shape[1]
    padded = rows + 2 * LEAD
    codes = (own[...].astype(f32) + near[...].astype(f32) + far[...].astype(f32))[0:8]
    hot = one_hot(codes, lanes, LEAD - 2)[:, :padded]
    hot = jnp.concatenate([hot, hot, hot], axis=0)
    stem[...] = lax.dot_general(
        hot, weight[...], (((0,), (0,)), ((), ())), preferred_element_type=f32
    )
    mine = one_hot(codes, lanes, lanes - 2)
    first = lax.axis_index("context") * rows
    for edge in (0, LEAD + rows):
        act = 0.5 * (
            gelu_tanh(stem[edge : edge + LEAD, :width]) + gelu_tanh(stem[edge : edge + LEAD, width:])
        )
        act = act.astype(bf16).astype(f32)
        spot = first - LEAD + edge + lax.broadcasted_iota(jnp.int32, (LEAD, 1), 0)
        inside = (spot >= 0) & (spot < total)
        gated[edge : edge + LEAD, :] = jnp.where(inside, gelu_tanh(act), 0.0).astype(bf16)
    top, end = edges[0:8, :], edges[8:16, :]
    none = jnp.zeros((24, width), f32)
    step = 32
    for r in range(0, rows, step):
        even = stem[LEAD + r : LEAD + r + step, :width]
        odd = stem[LEAD + r : LEAD + r + step, width:]
        even, even_slope = gelu_both(even)
        odd, odd_slope = gelu_both(odd)
        low = (0.5 * (even + odd)).astype(bf16)
        pooled[r : r + step, :] = low
        gate, slope = gelu_both(low.astype(f32))
        gated[LEAD + r : LEAD + r + step, :] = gate.astype(bf16)
        rise = back[r : r + step, :]
        if r == 0:
            rise = rise + jnp.concatenate([top, none], axis=0)
        if r + step == rows:
            rise = rise + jnp.concatenate([none, end], axis=0)
        grad = cot[r : r + step, :].astype(f32) + rise * slope
        d_pooled[r : r + step, :] = grad.astype(bf16)
        half = 0.5 * grad
        stem[LEAD + r : LEAD + r + step, :width] = half * even_slope
        stem[LEAD + r : LEAD + r + step, width:] = half * odd_slope
    grads = jnp.dot(
        mine[:, :rows], stem[LEAD : LEAD + rows, :].astype(bf16), preferred_element_type=f32
    )
    even, odd = orders(stem_part.shape[0] // 4 - 1)
    for k in range(len(even) - 1):
        for a in range(4):
            p, q = 16 * a + even.index(k), 16 * a + odd.index(k)
            stem_part[4 * k + a : 4 * k + a + 1, :] = (
                grads[p : p + 1, :width] + grads[q : q + 1, width:]
            )
    stem_part[stem_part.shape[0] - 4 :, :] = jnp.zeros((4, width), f32)


def feature_kernel(rows, gated, pooled, conv, out):
    acc = pooled[...].astype(f32)
    for t in range(TAPS):
        start = LEAD - 2 + t
        acc = acc + jnp.dot(gated[start : start + rows, :], conv[t], preferred_element_type=f32)
    out[...] = acc.astype(bf16)


def put_pieces(pieces, out, room, sems):
    ctx, core, y = place_of()
    unit = room.shape[1]
    half = out.shape[1] // 2
    copies = []
    at = 0
    for piece, chain, flip, ids in pieces:
        tap, taps = ((0, FIRST), (FIRST, TAPS - FIRST))[chain]
        from_core = lax.rem(core + flip, 2)
        q = quarter_bit(ctx, from_core)
        for k, p in enumerate(ids):
            dq = jnp.where(from_core == 0, p % 2, p // 2)
            dy = jnp.where(from_core == 0, p // 2, p % 2)
            from_q, from_y = lax.rem(q + dq, 2), lax.rem(y + dy, 2)
            channel = from_y * half + (2 * from_core + from_q) * unit
            for t in range(taps):
                low = (k * taps + t) * unit
                room[at + t] = piece[low : low + unit, :].astype(f32)
            copy = pltpu.make_async_copy(
                room.at[pl.ds(at, taps)],
                out.at[pl.ds(tap, taps), pl.ds(pl.multiple_of(channel, 16), unit)],
                sems.at[len(copies)],
            )
            copy.start()
            copies.append(copy)
            at += taps
    return copies


def early_kernel(left, right, got_left, got_right, out, room, sems):
    pieces = [(left, 0, 0), (right, 1, 0), (got_left, 0, 1), (got_right, 1, 1)]
    for copy in put_pieces([(*piece, (0, 1)) for piece in pieces], out, room, sems):
        copy.wait()


def late_kernel(left, right, got_left, whole, out, room, sems):
    del whole
    pieces = [(left, 0, 0, (2, 3)), (right, 1, 0, (2, 3)), (got_left, 0, 1, (2, 3))]
    for copy in put_pieces(pieces, out, room, sems):
        copy.wait()


def last_kernel(right, stem, whole, out, stem_out, room, sems, stem_v, stem_sem):
    del whole
    mine = stem[...].astype(bf16).astype(f32)
    total = mine + right[right.shape[0] - stem.shape[0] :, :].astype(f32)
    for k in range(stem_out.shape[0]):
        stem_v[k] = total[4 * k : 4 * k + 4, :]
    copy = pltpu.make_async_copy(stem_v, stem_out, stem_sem)
    copy.start()
    copies = put_pieces([(right, 1, 1, (2, 3))], out, room, sems)
    for done in [*copies, copy]:
        done.wait()


def per_device(codes, variant_pos, variant_shift, stem_weight, conv_weight, cotangent):
    n_dp, n_ctx = lax.axis_size("dp"), lax.axis_size("context")
    devices = n_dp * n_ctx
    length = codes.shape[1]
    rows = length // 2
    taps, _, width = stem_weight.shape
    half = width // 2
    unit = half // 4
    total = rows * n_ctx
    lanes = -(-(rows + 256) // 128) * 128
    core = lax.axis_index("context") % 2
    cot = cotangent[0]
    z_bit, y_bit = 2, n_ctx
    x_bit = 4 if n_ctx % 8 == 0 else 2

    def swap(value, even_bit, odd_bit=None):
        odd_bit = even_bit if odd_bit is None else odd_bit
        pairs = [(i, i ^ (odd_bit if i & 1 else even_bit)) for i in range(devices)]
        return lax.ppermute(value, AXES, pairs)

    def call(kernel, out, operands, scratch=(), keep=(), **options):
        if keep:
            options["input_output_aliases"] = {
                len(operands) + k: len(out) + k for k in range(len(keep))
            }
            kernel = holding(kernel, len(operands), len(out), len(keep))
            operands = list(operands) + near_by(*keep)
            out = list(out) + [(value.shape, value.dtype) for value in keep]
        shapes = [jax.ShapeDtypeStruct(o[0], o[1]) for o in out]
        specs = [o[2] if len(o) > 2 else VMEM for o in out]
        options.setdefault("compiler_params", params())
        return pl.pallas_call(
            kernel,
            out_shape=shapes,
            in_specs=[spec for _, spec in operands],
            out_specs=specs,
            scratch_shapes=list(scratch),
            **options,
        )(*[value for value, _ in operands])

    def near_by(*values):
        return [(value, VMEM) for value in values]

    def far_off(*values):
        return [(pltpu.with_memory_space_constraint(value, pltpu.HBM), FAR) for value in values]

    outward = {}
    for d in range(n_dp):
        for c in range(n_ctx):
            other = c + 1 if c & 1 else c - 1
            if 0 <= other < n_ctx:
                outward[d * n_ctx + c] = d * n_ctx + other

    pair_cot = swap(cot, y_bit)
    dma = pltpu.SemaphoreType.DMA
    edge = ((16, lanes), bf16)
    own, near, far = call(
        functools.partial(first_kernel, rows, lanes),
        [edge, edge, edge],
        far_off(codes, variant_pos, variant_shift, cot),
        [
            pltpu.VMEM((1, length), jnp.int32),
            pltpu.SMEM(variant_pos.shape, jnp.int32),
            pltpu.SMEM(variant_pos.shape, jnp.int32),
            pltpu.VMEM((16, width), bf16),
            pltpu.VMEM((16, width), bf16),
            dma((5,)),
        ],
        compiler_params=params(FIRST_LIMIT),
    )
    weight, half_weight, cot_v, conv_v = call(
        second_kernel,
        [
            ((192, 2 * width), bf16),
            ((192, width), bf16),
            (cot.shape, bf16),
            (conv_weight.shape, bf16),
        ],
        far_off(cot, stem_weight, conv_weight) + near_by(near),
        [pltpu.VMEM(stem_weight.shape, f32), dma((3,))],
    )
    near = swap(near, 1)
    cost = pl.CostEstimate(
        flops=2 * TAPS * rows * width * width, bytes_accessed=4 << 20, transcendentals=0
    )
    padded = rows + 2 * LEAD
    far = lax.ppermute(far, AXES, list(outward.items()))
    pair_codes = swap(own + near + far, y_bit)
    stem_half = pltpu.VMEM((width, rows + 128), f32)
    gates = ((TAPS * half, rows), bf16)
    part, edges = call(
        functools.partial(own_kernel, rows, total),
        [((TAPS * half, width), f32), ((16, width), f32)],
        near_by(own, near, far, half_weight, conv_v, cot_v),
        [stem_half, pltpu.VMEM(*gates)],
    )
    (pair_gates,) = call(
        functools.partial(pair_kernel, rows, total),
        [gates],
        near_by(pair_codes, half_weight),
        [stem_half],
    )
    size = TAPS * half // 2
    sent, kept = call(
        sum_kernel,
        [((size, width), bf16), ((size, width), f32)],
        near_by(part, pair_gates, pair_cot),
    )
    got = swap(sent, 1)
    (back,) = call(
        functools.partial(back_kernel, rows),
        [((rows, width), f32)],
        near_by(conv_v, after(cot_v, sent)),
        [pltpu.VMEM((padded, width), bf16)],
        cost_estimate=cost,
    )
    got, back = lax.optimization_barrier((got, back))
    size //= 2
    sent, kept, back = call(
        split_kernel,
        [((size, width), bf16), ((size, width), f32)],
        near_by(kept, got),
        keep=[back],
    )
    got = swap(sent, x_bit, z_bit)
    d_pooled, stem_part, gated, pooled = call(
        functools.partial(slope_kernel, rows, total),
        [
            ((rows, width), bf16),
            ((4 * taps + 4, width), f32),
            ((padded, width), bf16),
            ((rows, width), bf16),
        ],
        near_by(after(own, sent), near, far, weight, back, edges, cot_v),
        [pltpu.VMEM((padded, 2 * width), f32)],
        cost_estimate=cost,
    )
    value = kept + got.astype(f32)

    cut = FIRST * unit
    rest = size - cut
    left = value[:cut]
    right = jnp.concatenate([value[cut:], stem_part], axis=0)
    bits = [1 << k for k in range(devices.bit_length() - 1)]
    even_rest = [b for b in bits if b not in (1, x_bit, y_bit)]
    odd_rest = [b for b in bits if b not in (1, z_bit, y_bit)]
    odd_rest = odd_rest[1:] + odd_rest[:1]
    for k, (b, odd_b) in enumerate(zip(even_rest, odd_rest)):
        left, right = rounded(left), rounded(right)
        if k == 0:
            pooled = after(pooled, right.astype(bf16))
        left, right = [v + swap(v.astype(bf16), b, odd_b).astype(f32) for v in (left, right)]
    (features,) = call(
        functools.partial(feature_kernel, rows),
        [((rows, width), bf16)],
        near_by(gated, pooled, conv_v),
        cost_estimate=cost,
    )
    left, features = together(left, features)
    left = left.astype(bf16)
    stem_sum = right[rest:]
    right = right[:rest].astype(bf16)

    whole = ((TAPS, width, width), f32, FAR)

    def joined(pieces):
        return jnp.concatenate([pieces, stem_sum.astype(bf16)], axis=0)

    stem_sum = rounded(stem_sum)
    got_left, got_right = swap(left, x_bit, y_bit), swap(joined(right), x_bit, y_bit)
    left = jnp.concatenate([left, got_left], axis=0)
    stem_sum = stem_sum + got_right[rest:].astype(f32)
    right = jnp.concatenate([right, got_right[:rest]], axis=0)

    stem_sum = rounded(stem_sum)
    got_left, got_right = swap(left, y_bit, z_bit), swap(joined(right), y_bit, z_bit)
    (conv_grad,) = call(
        early_kernel,
        [whole],
        near_by(left, right, swap(left, 1), swap(right, 1)),
        [pltpu.VMEM((TAPS * 4, unit, width), f32), dma((8,))],
    )
    stem_sum = stem_sum + got_right[2 * rest :].astype(f32)
    left, right = got_left, got_right[: 2 * rest]
    left, conv_grad = together(left, conv_grad)
    got_left, got_right = swap(left, 1), swap(joined(right), 1)
    (conv_grad,) = call(
        late_kernel,
        [whole],
        near_by(left, right, got_left) + far_off(conv_grad),
        [pltpu.VMEM((2 * (TAPS + FIRST), unit, width), f32), dma((6,))],
        input_output_aliases={3: 0},
    )
    conv_grad, stem_grad = call(
        last_kernel,
        [whole, (stem_weight.shape, f32, FAR)],
        near_by(got_right, stem_sum) + far_off(conv_grad),
        [
            pltpu.VMEM((2 * (TAPS - FIRST), unit, width), f32),
            dma((2,)),
            pltpu.VMEM(stem_weight.shape, f32),
            dma,
        ],
        input_output_aliases={2: 0},
    )
    return (features[None], d_pooled[None], conv_grad, stem_grad)


def solution(mesh):
    placed = (P("dp", "context"), P("dp", None), P("dp", None), P(), P(), P("dp", "context", None))
    return jax.shard_map(
        per_device,
        mesh=mesh,
        in_specs=placed,
        out_specs=(P("dp", "context", None), P("dp", "context", None), P(), P()),
        check_vma=False,
    )
```

```python
import functools
import math

import jax
import jax.numpy as jnp
from jax import lax
from jax.experimental import pallas as pl
from jax.experimental.pallas import tpu as pltpu
from jax.sharding import PartitionSpec as P

root_scale = math.sqrt(2.0 / math.pi)
cubic = 0.044715
AXES = ("dp", "context")
TAPS = 5
FIRST = 3
FIRST_LIMIT = 48
HALO = 6
LEAD = 16
VMEM = pl.BlockSpec(memory_space=pltpu.VMEM)
FAR = pl.BlockSpec(memory_space=pltpu.HBM)
bf16 = jnp.bfloat16
f32 = jnp.float32


def gelu_tanh(value):
    inner = jnp.tanh(value * (root_scale + (root_scale * cubic) * (value * value)))
    half = 0.5 * value
    return half + half * inner


def gelu_both(value):
    square = value * value
    inner = jnp.tanh(value * (root_scale + (root_scale * cubic) * square))
    rise = (1.0 - inner * inner) * (root_scale + (3.0 * root_scale * cubic) * square)
    half = 0.5 * value
    return half + half * inner, 0.5 + 0.5 * inner + half * rise


def rounded(value):
    return lax.reduce_precision(value, 8, 7)


def params(limit=24):
    return pltpu.CompilerParams(vmem_limit_bytes=limit * 1024 * 1024)


def together(*values):
    return lax.optimization_barrier(values)


def after(value, *others):
    return together(value, *others)[0]


def holding(kernel, operands, results, kept):
    def run(*refs):
        last = operands + kept + results
        kernel(*refs[:operands], *refs[operands + kept : last], *refs[last + kept :])

    return run


def first_kernel(
    rows,
    lanes,
    codes,
    positions,
    amounts,
    cot,
    own,
    near,
    far,
    base_v,
    pos_s,
    amt_s,
    top,
    bottom,
    sems,
):
    length = 2 * rows
    tiles = length // 128
    width = cot.shape[1]
    copies = [
        pltpu.make_async_copy(codes, base_v, sems.at[0]),
        pltpu.make_async_copy(positions, pos_s, sems.at[1]),
        pltpu.make_async_copy(amounts, amt_s, sems.at[2]),
        pltpu.make_async_copy(cot.at[pl.ds(0, 16)], top, sems.at[3]),
        pltpu.make_async_copy(cot.at[pl.ds(rows - 16, 16)], bottom, sems.at[4]),
    ]
    for copy in copies:
        copy.start()
    ctx = lax.axis_index("context")
    core = lax.rem(ctx, 2)
    for copy in copies:
        copy.wait()
    x = jnp.concatenate([base_v[:, 128 * q : 128 * q + 128] for q in range(tiles)], axis=0)
    spot = (
        ctx * length
        + 128 * lax.broadcasted_iota(jnp.int32, x.shape, 0)
        + lax.broadcasted_iota(jnp.int32, x.shape, 1)
    )
    sums = [x] + [jnp.zeros_like(x)] * 3
    for v in range(positions.shape[1]):
        sums[v % 4] = sums[v % 4] + jnp.where(spot == pos_s[0, v], amt_s[0, v], 0)
    x = (sums[0] + sums[1]) + (sums[2] + sums[3])
    x = ((x & 3) + 1).astype(f32).astype(bf16)
    source = lax.broadcasted_iota(jnp.int32, (128, 128), 0)
    target = lax.broadcasted_iota(jnp.int32, (128, 128), 1)

    def picked(parity):
        left = (source == 2 * target + parity).astype(f32).astype(bf16)
        right = (source == 2 * (target - 64) + parity).astype(f32).astype(bf16)
        low = jnp.dot(x, left, preferred_element_type=f32)
        high = jnp.dot(x, right, preferred_element_type=f32)
        parts = [low[2 * q : 2 * q + 1] + high[2 * q + 1 : 2 * q + 2] for q in range(tiles // 2)]
        return jnp.concatenate(parts + [jnp.zeros((1, lanes - rows), f32)], axis=1)

    both = jnp.concatenate([picked(0), picked(1), jnp.zeros((6, lanes), f32)], axis=0)
    lane = lax.broadcasted_iota(jnp.int32, both.shape, 1)
    shifted = pltpu.roll(both, HALO, 1)
    last = jnp.where(lane < HALO, pltpu.roll(both, lanes - (rows - HALO), 1), 0.0)
    ahead = (lane >= rows + HALO) & (lane < rows + 2 * HALO)
    first = jnp.where(ahead, pltpu.roll(both, rows + HALO, 1), 0.0)
    blank = jnp.zeros((8, lanes), f32)
    pad = jnp.zeros((2, lanes - width), f32)

    def message(edge, grads):
        grads = jnp.concatenate([grads, pad], axis=1)
        return jnp.concatenate([edge, grads, jnp.zeros((6, lanes), f32)], axis=0)

    head = message(first, top[...].astype(f32)[0:2])
    tail = message(last, bottom[...].astype(f32)[14:16])
    own[...] = jnp.concatenate([shifted, blank], axis=0).astype(bf16)
    near[...] = jnp.where(core == 0, tail, head).astype(bf16)
    far[...] = jnp.where(core == 0, head, tail).astype(bf16)


def second_kernel(
    cot, stem_weight, conv, near, weight, half_weight, cot_out, conv_out, weight_v, sems
):
    del near
    copies = [
        pltpu.make_async_copy(stem_weight, weight_v, sems.at[0]),
        pltpu.make_async_copy(cot, cot_out, sems.at[1]),
        pltpu.make_async_copy(conv, conv_out, sems.at[2]),
    ]
    for copy in copies:
        copy.start()
    copies[0].wait()
    stem_terms(weight_v, weight, half_weight)
    for copy in copies[1:]:
        copy.wait()


def stem_terms(weight, out, half_out):
    width = weight.shape[2]
    zero = jnp.zeros((1, width), f32)
    even, odd = orders(weight.shape[0])

    def rows(order):
        return jnp.concatenate(
            [
                zero if k is None else weight[k, a : a + 1, :]
                for a in range(4)
                for k in order
            ],
            axis=0,
        )

    def terms(full):
        high = full.astype(bf16)
        left = full - high.astype(f32)
        middle = left.astype(bf16)
        low = (left - middle.astype(f32)).astype(bf16)
        return jnp.concatenate([high, middle, low], axis=0)

    evens, odds = rows(even), rows(odd)
    half = width // 2
    upper = lax.rem(lax.axis_index("dp"), 2) == 1
    out[...] = terms(jnp.concatenate([evens, odds], axis=1))
    mine = [jnp.where(upper, v[:, half:], v[:, :half]) for v in (evens, odds)]
    half_out[...] = terms(jnp.concatenate(mine, axis=1))


def orders(taps):
    even = [None] + list(range(taps - 2, 0, -2)) + list(range(taps - 1, -1, -2))
    odd = list(range(taps - 1, -1, -2)) + list(range(taps - 2, 0, -2)) + [None]
    return even, odd


def one_hot(codes, lanes, shift):
    even = jnp.broadcast_to(codes[0:1], (8, lanes))
    odd = jnp.broadcast_to(codes[1:2], (8, lanes))
    even = pltpu.roll(even, (2 * lanes - 8 + shift) % lanes, 1, stride=1, stride_axis=0)
    odd = pltpu.roll(odd, (2 * lanes - 7 + shift) % lanes, 1, stride=1, stride_axis=0)
    near = jnp.concatenate([even, odd], axis=0)
    return jnp.concatenate([(near == a + 1.0).astype(f32) for a in range(4)], axis=0).astype(bf16)


def shifted_gates(codes, first, total, weight, rows, stem, gated):
    used = rows + 128
    half = weight.shape[1] // 2
    quarter = half // 4
    hot = one_hot(codes, codes.shape[1], 0)[:, :used]
    hot = jnp.concatenate([hot, hot, hot], axis=0)
    stem[...] = lax.dot_general(
        weight[...], hot, (((0,), (0,)), ((), ())), preferred_element_type=f32
    )
    spot = first - 2 + lax.broadcasted_iota(jnp.int32, (1, used), 1)
    inside = (spot >= 0) & (spot < total)
    step = 16
    for c in range(0, half, step):
        even = gelu_tanh(stem[c : c + step, :])
        odd = gelu_tanh(stem[half + c : half + c + step, :])
        pooled = (0.5 * (even + odd)).astype(bf16).astype(f32)
        value = jnp.where(inside, gelu_tanh(pooled), 0.0)
        for t in range(TAPS):
            moved = value if t == 0 else pltpu.roll(value, used - t, 1)
            at = (c // quarter * TAPS + t) * quarter + c % quarter
            gated[at : at + step, :] = moved[:, :rows].astype(bf16)


def own_kernel(rows, total, own, near, far, weight, conv, cot, out, edges, stem, gated):
    first = lax.axis_index("context") * rows
    codes = (own[...].astype(f32) + near[...].astype(f32) + far[...].astype(f32))[0:8]
    shifted_gates(codes, first, total, weight, rows, stem, gated)
    edges[...] = edge_terms(near, far, conv)
    out[...] = jnp.dot(gated[...], cot[...], preferred_element_type=f32)


def pair_kernel(rows, total, codes, weight, gated, stem):
    first = lax.axis_index("context") * rows
    shifted_gates(codes[...].astype(f32)[0:8], first, total, weight, rows, stem, gated)


def sum_kernel(other, part, gated, cot, out):
    core = lax.rem(lax.axis_index("context"), 2)
    which = 1 - core if other else core
    size = out.shape[0]
    span = pl.ds(pl.multiple_of(which * size, 16), size)
    value = part[span, :] + jnp.dot(gated[span, :], cot[...], preferred_element_type=f32)
    out[...] = value.astype(out.dtype)


def place_of():
    ctx = lax.axis_index("context")
    return ctx, lax.rem(ctx, 2), lax.rem(lax.axis_index("dp"), 2)


def quarter_bit(ctx, core):
    far = 4 if lax.axis_size("context") % 8 == 0 else 2
    return jnp.where(core == 0, lax.rem(ctx // far, 2), lax.rem(ctx // 2, 2))


def split_kernel(value, got, sent, kept):
    x = quarter_bit(*place_of()[:2])
    size = sent.shape[0]
    for which, out in ((1 - x, sent), (x, kept)):
        span = pl.ds(pl.multiple_of(which * size, 16), size)
        out[...] = (value[span, :] + got[span, :].astype(f32)).astype(out.dtype)


def back_kernel(rows, conv, cot, back, ext):
    width = cot.shape[1]
    blank = jnp.zeros((LEAD, width), bf16)
    ext[0:LEAD, :] = blank
    ext[LEAD : LEAD + rows, :] = cot[...]
    ext[LEAD + rows :, :] = blank
    for t in range(TAPS):
        start = LEAD + 2 - t
        term = turned(ext[start : start + rows, :], conv[t])
        back[...] = term if t == 0 else back[...] + term


def turned(left, right):
    return lax.dot_general(left, right, (((1,), (1,)), ((), ())), preferred_element_type=f32)


def edge_terms(near, far, conv):
    width = conv.shape[1]
    core = lax.rem(lax.axis_index("context"), 2)
    near_v, far_v = near[...].astype(f32), far[...].astype(f32)
    before = jnp.where(core == 0, far_v, near_v)[8:10, :width]
    behind = jnp.where(core == 0, near_v, far_v)[8:10, :width]
    none = jnp.zeros((6, width), f32)
    one = jnp.zeros((1, width), f32)
    top = jnp.concatenate([before, none], axis=0).astype(bf16)
    top_late = jnp.concatenate([before[1:2], one, none], axis=0).astype(bf16)
    end = jnp.concatenate([none, behind], axis=0).astype(bf16)
    end_late = jnp.concatenate([none, one, behind[0:1]], axis=0).astype(bf16)
    first = turned(top, conv[4]) + turned(top_late, conv[3])
    last = turned(end, conv[0]) + turned(end_late, conv[1])
    return jnp.concatenate([first, last], axis=0)


def slope_kernel(
    rows, total, own, near, far, weight, back, edges, cot, d_pooled, stem_part, gated, pooled, stem
):
    lanes = own.shape[1]
    width = cot.shape[1]
    padded = rows + 2 * LEAD
    codes = (own[...].astype(f32) + near[...].astype(f32) + far[...].astype(f32))[0:8]
    hot = one_hot(codes, lanes, LEAD - 2)[:, :padded]
    hot = jnp.concatenate([hot, hot, hot], axis=0)
    stem[...] = lax.dot_general(
        hot, weight[...], (((0,), (0,)), ((), ())), preferred_element_type=f32
    )
    mine = one_hot(codes, lanes, lanes - 2)
    first = lax.axis_index("context") * rows
    for edge in (0, LEAD + rows):
        act = 0.5 * (
            gelu_tanh(stem[edge : edge + LEAD, :width]) + gelu_tanh(stem[edge : edge + LEAD, width:])
        )
        act = act.astype(bf16).astype(f32)
        spot = first - LEAD + edge + lax.broadcasted_iota(jnp.int32, (LEAD, 1), 0)
        inside = (spot >= 0) & (spot < total)
        gated[edge : edge + LEAD, :] = jnp.where(inside, gelu_tanh(act), 0.0).astype(bf16)
    top, end = edges[0:8, :], edges[8:16, :]
    none = jnp.zeros((24, width), f32)
    step = 32
    for r in range(0, rows, step):
        even = stem[LEAD + r : LEAD + r + step, :width]
        odd = stem[LEAD + r : LEAD + r + step, width:]
        even, even_slope = gelu_both(even)
        odd, odd_slope = gelu_both(odd)
        low = (0.5 * (even + odd)).astype(bf16)
        pooled[r : r + step, :] = low
        gate, slope = gelu_both(low.astype(f32))
        gated[LEAD + r : LEAD + r + step, :] = gate.astype(bf16)
        rise = back[r : r + step, :]
        if r == 0:
            rise = rise + jnp.concatenate([top, none], axis=0)
        if r + step == rows:
            rise = rise + jnp.concatenate([none, end], axis=0)
        grad = cot[r : r + step, :].astype(f32) + rise * slope
        d_pooled[r : r + step, :] = grad.astype(bf16)
        half = 0.5 * grad
        stem[LEAD + r : LEAD + r + step, :width] = half * even_slope
        stem[LEAD + r : LEAD + r + step, width:] = half * odd_slope
    grads = jnp.dot(
        mine[:, :rows], stem[LEAD : LEAD + rows, :].astype(bf16), preferred_element_type=f32
    )
    even, odd = orders(stem_part.shape[0] // 4 - 1)
    for k in range(len(even) - 1):
        for a in range(4):
            p, q = 16 * a + even.index(k), 16 * a + odd.index(k)
            stem_part[4 * k + a : 4 * k + a + 1, :] = (
                grads[p : p + 1, :width] + grads[q : q + 1, width:]
            )
    stem_part[stem_part.shape[0] - 4 :, :] = jnp.zeros((4, width), f32)


def feature_kernel(rows, gated, pooled, conv, out):
    acc = pooled[...].astype(f32)
    for t in range(TAPS):
        start = LEAD - 2 + t
        acc = acc + jnp.dot(gated[start : start + rows, :], conv[t], preferred_element_type=f32)
    out[...] = acc.astype(bf16)


def put_pieces(pieces, out, room, sems):
    ctx, core, y = place_of()
    unit = room.shape[1]
    half = out.shape[1] // 2
    copies = []
    at = 0
    for piece, chain, flip, ids in pieces:
        tap, taps = ((0, FIRST), (FIRST, TAPS - FIRST))[chain]
        from_core = lax.rem(core + flip, 2)
        q = quarter_bit(ctx, from_core)
        for k, p in enumerate(ids):
            dq = jnp.where(from_core == 0, p % 2, p // 2)
            dy = jnp.where(from_core == 0, p // 2, p % 2)
            from_q, from_y = lax.rem(q + dq, 2), lax.rem(y + dy, 2)
            channel = from_y * half + (2 * from_core + from_q) * unit
            for t in range(taps):
                low = (k * taps + t) * unit
                room[at + t] = piece[low : low + unit, :].astype(f32)
            copy = pltpu.make_async_copy(
                room.at[pl.ds(at, taps)],
                out.at[pl.ds(tap, taps), pl.ds(pl.multiple_of(channel, 16), unit)],
                sems.at[len(copies)],
            )
            copy.start()
            copies.append(copy)
            at += taps
    return copies


def early_kernel(left, right, got_left, got_right, out, room, sems):
    pieces = [(left, 0, 0), (right, 1, 0), (got_left, 0, 1), (got_right, 1, 1)]
    for copy in put_pieces([(*piece, (0, 1)) for piece in pieces], out, room, sems):
        copy.wait()


def late_kernel(left, right, got_left, whole, out, room, sems):
    del whole
    pieces = [(left, 0, 0, (2, 3)), (right, 1, 0, (2, 3)), (got_left, 0, 1, (2, 3))]
    for copy in put_pieces(pieces, out, room, sems):
        copy.wait()


def last_kernel(right, stem, whole, out, stem_out, room, sems, stem_v, stem_sem):
    del whole
    mine = stem[...].astype(bf16).astype(f32)
    total = mine + right[right.shape[0] - stem.shape[0] :, :].astype(f32)
    for k in range(stem_out.shape[0]):
        stem_v[k] = total[4 * k : 4 * k + 4, :]
    copy = pltpu.make_async_copy(stem_v, stem_out, stem_sem)
    copy.start()
    copies = put_pieces([(right, 1, 1, (2, 3))], out, room, sems)
    for done in [*copies, copy]:
        done.wait()


def per_device(codes, variant_pos, variant_shift, stem_weight, conv_weight, cotangent):
    n_dp, n_ctx = lax.axis_size("dp"), lax.axis_size("context")
    devices = n_dp * n_ctx
    length = codes.shape[1]
    rows = length // 2
    taps, _, width = stem_weight.shape
    half = width // 2
    unit = half // 4
    total = rows * n_ctx
    lanes = -(-(rows + 256) // 128) * 128
    cot = cotangent[0]
    z_bit, y_bit = 2, n_ctx
    x_bit = 4 if n_ctx % 8 == 0 else 2

    def swap(value, even_bit, odd_bit=None):
        odd_bit = even_bit if odd_bit is None else odd_bit
        pairs = [(i, i ^ (odd_bit if i & 1 else even_bit)) for i in range(devices)]
        return lax.ppermute(value, AXES, pairs)

    def call(kernel, out, operands, scratch=(), keep=(), **options):
        if keep:
            options["input_output_aliases"] = {
                len(operands) + k: len(out) + k for k in range(len(keep))
            }
            kernel = holding(kernel, len(operands), len(out), len(keep))
            operands = list(operands) + near_by(*keep)
            out = list(out) + [(value.shape, value.dtype) for value in keep]
        shapes = [jax.ShapeDtypeStruct(o[0], o[1]) for o in out]
        specs = [o[2] if len(o) > 2 else VMEM for o in out]
        options.setdefault("compiler_params", params())
        return pl.pallas_call(
            kernel,
            out_shape=shapes,
            in_specs=[spec for _, spec in operands],
            out_specs=specs,
            scratch_shapes=list(scratch),
            **options,
        )(*[value for value, _ in operands])

    def near_by(*values):
        return [(value, VMEM) for value in values]

    def far_off(*values):
        return [(pltpu.with_memory_space_constraint(value, pltpu.HBM), FAR) for value in values]

    outward = {}
    for d in range(n_dp):
        for c in range(n_ctx):
            other = c + 1 if c & 1 else c - 1
            if 0 <= other < n_ctx:
                outward[d * n_ctx + c] = d * n_ctx + other

    pair_cot = swap(cot, y_bit)
    dma = pltpu.SemaphoreType.DMA
    edge = ((16, lanes), bf16)
    own, near, far = call(
        functools.partial(first_kernel, rows, lanes),
        [edge, edge, edge],
        far_off(codes, variant_pos, variant_shift, cot),
        [
            pltpu.VMEM((1, length), jnp.int32),
            pltpu.SMEM(variant_pos.shape, jnp.int32),
            pltpu.SMEM(variant_pos.shape, jnp.int32),
            pltpu.VMEM((16, width), bf16),
            pltpu.VMEM((16, width), bf16),
            dma((5,)),
        ],
        compiler_params=params(FIRST_LIMIT),
    )
    weight, half_weight, cot_v, conv_v = call(
        second_kernel,
        [
            ((192, 2 * width), bf16),
            ((192, width), bf16),
            (cot.shape, bf16),
            (conv_weight.shape, bf16),
        ],
        far_off(cot, stem_weight, conv_weight) + near_by(near),
        [pltpu.VMEM(stem_weight.shape, f32), dma((3,))],
    )
    near = swap(near, 1)
    cost = pl.CostEstimate(
        flops=2 * TAPS * rows * width * width, bytes_accessed=4 << 20, transcendentals=0
    )
    padded = rows + 2 * LEAD
    far = lax.ppermute(far, AXES, list(outward.items()))
    pair_codes = swap(own + near + far, y_bit)
    stem_half = pltpu.VMEM((width, rows + 128), f32)
    gates = ((TAPS * half, rows), bf16)
    part, edges = call(
        functools.partial(own_kernel, rows, total),
        [((TAPS * half, width), f32), ((16, width), f32)],
        near_by(own, near, far, half_weight, conv_v, cot_v),
        [stem_half, pltpu.VMEM(*gates)],
    )
    (pair_gates,) = call(
        functools.partial(pair_kernel, rows, total),
        [gates],
        near_by(pair_codes, half_weight),
        [stem_half],
    )
    size = TAPS * half // 2
    (sent,) = call(
        functools.partial(sum_kernel, True),
        [((size, width), bf16)],
        near_by(part, pair_gates, pair_cot),
    )
    got = swap(sent, 1)
    (kept,) = call(
        functools.partial(sum_kernel, False),
        [((size, width), f32)],
        near_by(after(part, sent), pair_gates, pair_cot),
    )
    (back,) = call(
        functools.partial(back_kernel, rows),
        [((rows, width), f32)],
        near_by(conv_v, after(cot_v, sent)),
        [pltpu.VMEM((padded, width), bf16)],
        cost_estimate=cost,
    )
    got, back = lax.optimization_barrier((got, back))
    size //= 2
    sent, kept, back = call(
        split_kernel,
        [((size, width), bf16), ((size, width), f32)],
        near_by(kept, got),
        keep=[back],
    )
    got = swap(sent, x_bit, z_bit)
    d_pooled, stem_part, gated, pooled = call(
        functools.partial(slope_kernel, rows, total),
        [
            ((rows, width), bf16),
            ((4 * taps + 4, width), f32),
            ((padded, width), bf16),
            ((rows, width), bf16),
        ],
        near_by(after(own, sent), near, far, weight, back, edges, cot_v),
        [pltpu.VMEM((padded, 2 * width), f32)],
        cost_estimate=cost,
    )
    value = kept + got.astype(f32)

    cut = FIRST * unit
    rest = size - cut
    left = value[:cut]
    right = jnp.concatenate([value[cut:], stem_part], axis=0)
    bits = [1 << k for k in range(devices.bit_length() - 1)]
    even_rest = [b for b in bits if b not in (1, x_bit, y_bit)]
    odd_rest = [b for b in bits if b not in (1, z_bit, y_bit)]
    odd_rest = odd_rest[1:] + odd_rest[:1]
    for k, (b, odd_b) in enumerate(zip(even_rest, odd_rest)):
        left, right = rounded(left), rounded(right)
        if k == 0:
            pooled = after(pooled, right.astype(bf16))
        left, right = [v + swap(v.astype(bf16), b, odd_b).astype(f32) for v in (left, right)]
    (features,) = call(
        functools.partial(feature_kernel, rows),
        [((rows, width), bf16)],
        near_by(gated, pooled, conv_v),
        cost_estimate=cost,
    )
    left, features = together(left, features)
    left = left.astype(bf16)
    stem_sum = right[rest:]
    right = right[:rest].astype(bf16)

    whole = ((TAPS, width, width), f32, FAR)

    def joined(pieces):
        return jnp.concatenate([pieces, stem_sum.astype(bf16)], axis=0)

    stem_sum = rounded(stem_sum)
    got_left, got_right = swap(left, x_bit, y_bit), swap(joined(right), x_bit, y_bit)
    left = jnp.concatenate([left, got_left], axis=0)
    stem_sum = stem_sum + got_right[rest:].astype(f32)
    right = jnp.concatenate([right, got_right[:rest]], axis=0)

    stem_sum = rounded(stem_sum)
    got_left, got_right = swap(left, y_bit, z_bit), swap(joined(right), y_bit, z_bit)
    (conv_grad,) = call(
        early_kernel,
        [whole],
        near_by(left, right, swap(left, 1), swap(right, 1)),
        [pltpu.VMEM((TAPS * 4, unit, width), f32), dma((8,))],
    )
    stem_sum = stem_sum + got_right[2 * rest :].astype(f32)
    left, right = got_left, got_right[: 2 * rest]
    left, conv_grad = together(left, conv_grad)
    got_left, got_right = swap(left, 1), swap(joined(right), 1)
    (conv_grad,) = call(
        late_kernel,
        [whole],
        near_by(left, right, got_left) + far_off(conv_grad),
        [pltpu.VMEM((2 * (TAPS + FIRST), unit, width), f32), dma((6,))],
        input_output_aliases={3: 0},
    )
    conv_grad, stem_grad = call(
        last_kernel,
        [whole, (stem_weight.shape, f32, FAR)],
        near_by(got_right, stem_sum) + far_off(conv_grad),
        [
            pltpu.VMEM((2 * (TAPS - FIRST), unit, width), f32),
            dma((2,)),
            pltpu.VMEM(stem_weight.shape, f32),
            dma,
        ],
        input_output_aliases={2: 0},
    )
    return (features[None], d_pooled[None], conv_grad, stem_grad)


def solution(mesh):
    placed = (P("dp", "context"), P("dp", None), P("dp", None), P(), P(), P("dp", "context", None))
    return jax.shard_map(
        per_device,
        mesh=mesh,
        in_specs=placed,
        out_specs=(P("dp", "context", None), P("dp", "context", None), P(), P()),
        check_vma=False,
    )
```

```python
import functools
import math

import jax
import jax.numpy as jnp
from jax import lax
from jax.experimental import pallas as pl
from jax.experimental.pallas import tpu as pltpu
from jax.sharding import PartitionSpec as P

root_scale = math.sqrt(2.0 / math.pi)
cubic = 0.044715
AXES = ("dp", "context")
TAPS = 5
FIRST = 3
FIRST_LIMIT = 48
HALO = 6
LEAD = 16
VMEM = pl.BlockSpec(memory_space=pltpu.VMEM)
FAR = pl.BlockSpec(memory_space=pltpu.HBM)
bf16 = jnp.bfloat16
f32 = jnp.float32


def gelu_tanh(value):
    inner = jnp.tanh(value * (root_scale + (root_scale * cubic) * (value * value)))
    half = 0.5 * value
    return half + half * inner


def gelu_both(value):
    square = value * value
    inner = jnp.tanh(value * (root_scale + (root_scale * cubic) * square))
    rise = (1.0 - inner * inner) * (root_scale + (3.0 * root_scale * cubic) * square)
    half = 0.5 * value
    return half + half * inner, 0.5 + 0.5 * inner + half * rise


def rounded(value):
    return lax.reduce_precision(value, 8, 7)


def params(limit=24):
    return pltpu.CompilerParams(vmem_limit_bytes=limit * 1024 * 1024)


def together(*values):
    return lax.optimization_barrier(values)


def after(value, *others):
    return together(value, *others)[0]


def holding(kernel, operands, results, kept):
    def run(*refs):
        last = operands + kept + results
        kernel(*refs[:operands], *refs[operands + kept : last], *refs[last + kept :])

    return run


def first_kernel(
    rows,
    lanes,
    codes,
    positions,
    amounts,
    cot,
    own,
    near,
    far,
    base_v,
    pos_s,
    amt_s,
    top,
    bottom,
    sems,
):
    length = 2 * rows
    tiles = length // 128
    width = cot.shape[1]
    copies = [
        pltpu.make_async_copy(codes, base_v, sems.at[0]),
        pltpu.make_async_copy(positions, pos_s, sems.at[1]),
        pltpu.make_async_copy(amounts, amt_s, sems.at[2]),
        pltpu.make_async_copy(cot.at[pl.ds(0, 16)], top, sems.at[3]),
        pltpu.make_async_copy(cot.at[pl.ds(rows - 16, 16)], bottom, sems.at[4]),
    ]
    for copy in copies:
        copy.start()
    ctx = lax.axis_index("context")
    core = lax.rem(ctx, 2)
    for copy in copies:
        copy.wait()
    x = jnp.concatenate([base_v[:, 128 * q : 128 * q + 128] for q in range(tiles)], axis=0)
    spot = (
        ctx * length
        + 128 * lax.broadcasted_iota(jnp.int32, x.shape, 0)
        + lax.broadcasted_iota(jnp.int32, x.shape, 1)
    )
    sums = [x] + [jnp.zeros_like(x)] * 3
    for v in range(positions.shape[1]):
        sums[v % 4] = sums[v % 4] + jnp.where(spot == pos_s[0, v], amt_s[0, v], 0)
    x = (sums[0] + sums[1]) + (sums[2] + sums[3])
    x = ((x & 3) + 1).astype(f32).astype(bf16)
    source = lax.broadcasted_iota(jnp.int32, (128, 128), 0)
    target = lax.broadcasted_iota(jnp.int32, (128, 128), 1)

    def picked(parity):
        left = (source == 2 * target + parity).astype(f32).astype(bf16)
        right = (source == 2 * (target - 64) + parity).astype(f32).astype(bf16)
        low = jnp.dot(x, left, preferred_element_type=f32)
        high = jnp.dot(x, right, preferred_element_type=f32)
        parts = [low[2 * q : 2 * q + 1] + high[2 * q + 1 : 2 * q + 2] for q in range(tiles // 2)]
        return jnp.concatenate(parts + [jnp.zeros((1, lanes - rows), f32)], axis=1)

    both = jnp.concatenate([picked(0), picked(1), jnp.zeros((6, lanes), f32)], axis=0)
    lane = lax.broadcasted_iota(jnp.int32, both.shape, 1)
    shifted = pltpu.roll(both, HALO, 1)
    last = jnp.where(lane < HALO, pltpu.roll(both, lanes - (rows - HALO), 1), 0.0)
    ahead = (lane >= rows + HALO) & (lane < rows + 2 * HALO)
    first = jnp.where(ahead, pltpu.roll(both, rows + HALO, 1), 0.0)
    blank = jnp.zeros((8, lanes), f32)
    pad = jnp.zeros((2, lanes - width), f32)

    def message(edge, grads):
        grads = jnp.concatenate([grads, pad], axis=1)
        return jnp.concatenate([edge, grads, jnp.zeros((6, lanes), f32)], axis=0)

    head = message(first, top[...].astype(f32)[0:2])
    tail = message(last, bottom[...].astype(f32)[14:16])
    own[...] = jnp.concatenate([shifted, blank], axis=0).astype(bf16)
    near[...] = jnp.where(core == 0, tail, head).astype(bf16)
    far[...] = jnp.where(core == 0, head, tail).astype(bf16)


def second_kernel(
    cot, stem_weight, conv, near, weight, half_weight, cot_out, conv_out, weight_v, sems
):
    del near
    copies = [
        pltpu.make_async_copy(stem_weight, weight_v, sems.at[0]),
        pltpu.make_async_copy(cot, cot_out, sems.at[1]),
        pltpu.make_async_copy(conv, conv_out, sems.at[2]),
    ]
    for copy in copies:
        copy.start()
    copies[0].wait()
    stem_terms(weight_v, weight, half_weight)
    for copy in copies[1:]:
        copy.wait()


def stem_terms(weight, out, half_out):
    width = weight.shape[2]
    zero = jnp.zeros((1, width), f32)
    even, odd = orders(weight.shape[0])

    def rows(order):
        return jnp.concatenate(
            [
                zero if k is None else weight[k, a : a + 1, :]
                for a in range(4)
                for k in order
            ],
            axis=0,
        )

    def terms(full):
        high = full.astype(bf16)
        left = full - high.astype(f32)
        middle = left.astype(bf16)
        low = (left - middle.astype(f32)).astype(bf16)
        return jnp.concatenate([high, middle, low], axis=0)

    evens, odds = rows(even), rows(odd)
    half = width // 2
    upper = lax.rem(lax.axis_index("dp"), 2) == 1
    out[...] = terms(jnp.concatenate([evens, odds], axis=1))
    mine = [jnp.where(upper, v[:, half:], v[:, :half]) for v in (evens, odds)]
    half_out[...] = terms(jnp.concatenate(mine, axis=1))


def orders(taps):
    even = [None] + list(range(taps - 2, 0, -2)) + list(range(taps - 1, -1, -2))
    odd = list(range(taps - 1, -1, -2)) + list(range(taps - 2, 0, -2)) + [None]
    return even, odd


def one_hot(codes, lanes, shift):
    even = jnp.broadcast_to(codes[0:1], (8, lanes))
    odd = jnp.broadcast_to(codes[1:2], (8, lanes))
    even = pltpu.roll(even, (2 * lanes - 8 + shift) % lanes, 1, stride=1, stride_axis=0)
    odd = pltpu.roll(odd, (2 * lanes - 7 + shift) % lanes, 1, stride=1, stride_axis=0)
    near = jnp.concatenate([even, odd], axis=0)
    return jnp.concatenate([(near == a + 1.0).astype(f32) for a in range(4)], axis=0).astype(bf16)


def shifted_gates(codes, first, total, weight, rows, stem, gated):
    used = rows + 128
    half = weight.shape[1] // 2
    quarter = half // 4
    hot = one_hot(codes, codes.shape[1], 0)[:, :used]
    hot = jnp.concatenate([hot, hot, hot], axis=0)
    stem[...] = lax.dot_general(
        weight[...], hot, (((0,), (0,)), ((), ())), preferred_element_type=f32
    )
    spot = first - 2 + lax.broadcasted_iota(jnp.int32, (1, used), 1)
    inside = (spot >= 0) & (spot < total)
    step = 16
    for c in range(0, half, step):
        even = gelu_tanh(stem[c : c + step, :])
        odd = gelu_tanh(stem[half + c : half + c + step, :])
        pooled = (0.5 * (even + odd)).astype(bf16).astype(f32)
        value = jnp.where(inside, gelu_tanh(pooled), 0.0)
        for t in range(TAPS):
            moved = value if t == 0 else pltpu.roll(value, used - t, 1)
            at = (c // quarter * TAPS + t) * quarter + c % quarter
            gated[at : at + step, :] = moved[:, :rows].astype(bf16)


def own_kernel(rows, total, own, near, far, weight, conv, cot, out, edges, stem, gated):
    first = lax.axis_index("context") * rows
    codes = (own[...].astype(f32) + near[...].astype(f32) + far[...].astype(f32))[0:8]
    shifted_gates(codes, first, total, weight, rows, stem, gated)
    edges[...] = edge_terms(near, far, conv)
    out[...] = jnp.dot(gated[...], cot[...], preferred_element_type=f32)


def pair_kernel(rows, total, codes, weight, gated, stem):
    first = lax.axis_index("context") * rows
    shifted_gates(codes[...].astype(f32)[0:8], first, total, weight, rows, stem, gated)


def sum_kernel(other, part, gated, cot, out):
    core = lax.rem(lax.axis_index("context"), 2)
    which = 1 - core if other else core
    size = out.shape[0]
    span = pl.ds(pl.multiple_of(which * size, 16), size)
    value = part[span, :] + jnp.dot(gated[span, :], cot[...], preferred_element_type=f32)
    out[...] = value.astype(out.dtype)


def place_of():
    ctx = lax.axis_index("context")
    return ctx, lax.rem(ctx, 2), lax.rem(lax.axis_index("dp"), 2)


def quarter_bit(ctx, core):
    far = 4 if lax.axis_size("context") % 8 == 0 else 2
    return jnp.where(core == 0, lax.rem(ctx // far, 2), lax.rem(ctx // 2, 2))


def split_kernel(value, got, sent, kept):
    x = quarter_bit(*place_of()[:2])
    size = sent.shape[0]
    for which, out in ((1 - x, sent), (x, kept)):
        span = pl.ds(pl.multiple_of(which * size, 16), size)
        out[...] = (value[span, :] + got[span, :].astype(f32)).astype(out.dtype)


def back_kernel(rows, conv, cot, back, ext):
    width = cot.shape[1]
    blank = jnp.zeros((LEAD, width), bf16)
    ext[0:LEAD, :] = blank
    ext[LEAD : LEAD + rows, :] = cot[...]
    ext[LEAD + rows :, :] = blank
    terms = [
        turned(ext[LEAD + 2 - t : LEAD + 2 - t + rows, :], conv[t]) for t in range(TAPS)
    ]
    back[...] = sum(terms[1:], terms[0])


def turned(left, right):
    return lax.dot_general(left, right, (((1,), (1,)), ((), ())), preferred_element_type=f32)


def edge_terms(near, far, conv):
    width = conv.shape[1]
    core = lax.rem(lax.axis_index("context"), 2)
    near_v, far_v = near[...].astype(f32), far[...].astype(f32)
    before = jnp.where(core == 0, far_v, near_v)[8:10, :width]
    behind = jnp.where(core == 0, near_v, far_v)[8:10, :width]
    none = jnp.zeros((6, width), f32)
    one = jnp.zeros((1, width), f32)
    top = jnp.concatenate([before, none], axis=0).astype(bf16)
    top_late = jnp.concatenate([before[1:2], one, none], axis=0).astype(bf16)
    end = jnp.concatenate([none, behind], axis=0).astype(bf16)
    end_late = jnp.concatenate([none, one, behind[0:1]], axis=0).astype(bf16)
    first = turned(top, conv[4]) + turned(top_late, conv[3])
    last = turned(end, conv[0]) + turned(end_late, conv[1])
    return jnp.concatenate([first, last], axis=0)


def slope_kernel(
    rows, total, own, near, far, weight, back, edges, cot, d_pooled, stem_part, gated, pooled, stem
):
    lanes = own.shape[1]
    width = cot.shape[1]
    padded = rows + 2 * LEAD
    codes = (own[...].astype(f32) + near[...].astype(f32) + far[...].astype(f32))[0:8]
    hot = one_hot(codes, lanes, LEAD - 2)[:, :padded]
    hot = jnp.concatenate([hot, hot, hot], axis=0)
    stem[...] = lax.dot_general(
        hot, weight[...], (((0,), (0,)), ((), ())), preferred_element_type=f32
    )
    mine = one_hot(codes, lanes, lanes - 2)
    first = lax.axis_index("context") * rows
    for edge in (0, LEAD + rows):
        act = 0.5 * (
            gelu_tanh(stem[edge : edge + LEAD, :width]) + gelu_tanh(stem[edge : edge + LEAD, width:])
        )
        act = act.astype(bf16).astype(f32)
        spot = first - LEAD + edge + lax.broadcasted_iota(jnp.int32, (LEAD, 1), 0)
        inside = (spot >= 0) & (spot < total)
        gated[edge : edge + LEAD, :] = jnp.where(inside, gelu_tanh(act), 0.0).astype(bf16)
    top, end = edges[0:8, :], edges[8:16, :]
    none = jnp.zeros((24, width), f32)
    step = 32
    for r in range(0, rows, step):
        even = stem[LEAD + r : LEAD + r + step, :width]
        odd = stem[LEAD + r : LEAD + r + step, width:]
        even, even_slope = gelu_both(even)
        odd, odd_slope = gelu_both(odd)
        low = (0.5 * (even + odd)).astype(bf16)
        pooled[r : r + step, :] = low
        gate, slope = gelu_both(low.astype(f32))
        gated[LEAD + r : LEAD + r + step, :] = gate.astype(bf16)
        rise = back[r : r + step, :]
        if r == 0:
            rise = rise + jnp.concatenate([top, none], axis=0)
        if r + step == rows:
            rise = rise + jnp.concatenate([none, end], axis=0)
        grad = cot[r : r + step, :].astype(f32) + rise * slope
        d_pooled[r : r + step, :] = grad.astype(bf16)
        half = 0.5 * grad
        stem[LEAD + r : LEAD + r + step, :width] = half * even_slope
        stem[LEAD + r : LEAD + r + step, width:] = half * odd_slope
    grads = jnp.dot(
        mine[:, :rows], stem[LEAD : LEAD + rows, :].astype(bf16), preferred_element_type=f32
    )
    even, odd = orders(stem_part.shape[0] // 4 - 1)
    for k in range(len(even) - 1):
        for a in range(4):
            p, q = 16 * a + even.index(k), 16 * a + odd.index(k)
            stem_part[4 * k + a : 4 * k + a + 1, :] = (
                grads[p : p + 1, :width] + grads[q : q + 1, width:]
            )
    stem_part[stem_part.shape[0] - 4 :, :] = jnp.zeros((4, width), f32)


def feature_kernel(rows, gated, pooled, conv, out):
    acc = pooled[...].astype(f32)
    for t in range(TAPS):
        start = LEAD - 2 + t
        acc = acc + jnp.dot(gated[start : start + rows, :], conv[t], preferred_element_type=f32)
    out[...] = acc.astype(bf16)


def put_pieces(pieces, out, room, sems):
    ctx, core, y = place_of()
    unit = room.shape[1]
    half = out.shape[1] // 2
    copies = []
    at = 0
    for piece, chain, flip, ids in pieces:
        tap, taps = ((0, FIRST), (FIRST, TAPS - FIRST))[chain]
        from_core = lax.rem(core + flip, 2)
        q = quarter_bit(ctx, from_core)
        for k, p in enumerate(ids):
            dq = jnp.where(from_core == 0, p % 2, p // 2)
            dy = jnp.where(from_core == 0, p // 2, p % 2)
            from_q, from_y = lax.rem(q + dq, 2), lax.rem(y + dy, 2)
            channel = from_y * half + (2 * from_core + from_q) * unit
            for t in range(taps):
                low = (k * taps + t) * unit
                room[at + t] = piece[low : low + unit, :].astype(f32)
            copy = pltpu.make_async_copy(
                room.at[pl.ds(at, taps)],
                out.at[pl.ds(tap, taps), pl.ds(pl.multiple_of(channel, 16), unit)],
                sems.at[len(copies)],
            )
            copy.start()
            copies.append(copy)
            at += taps
    return copies


def early_kernel(left, right, got_left, got_right, out, room, sems):
    pieces = [(left, 0, 0), (right, 1, 0), (got_left, 0, 1), (got_right, 1, 1)]
    for copy in put_pieces([(*piece, (0, 1)) for piece in pieces], out, room, sems):
        copy.wait()


def late_kernel(left, right, got_left, whole, out, room, sems):
    del whole
    pieces = [(left, 0, 0, (2, 3)), (right, 1, 0, (2, 3)), (got_left, 0, 1, (2, 3))]
    for copy in put_pieces(pieces, out, room, sems):
        copy.wait()


def last_kernel(right, stem, whole, out, stem_out, room, sems, stem_v, stem_sem):
    del whole
    mine = stem[...].astype(bf16).astype(f32)
    total = mine + right[right.shape[0] - stem.shape[0] :, :].astype(f32)
    for k in range(stem_out.shape[0]):
        stem_v[k] = total[4 * k : 4 * k + 4, :]
    copy = pltpu.make_async_copy(stem_v, stem_out, stem_sem)
    copy.start()
    copies = put_pieces([(right, 1, 1, (2, 3))], out, room, sems)
    for done in [*copies, copy]:
        done.wait()


def per_device(codes, variant_pos, variant_shift, stem_weight, conv_weight, cotangent):
    n_dp, n_ctx = lax.axis_size("dp"), lax.axis_size("context")
    devices = n_dp * n_ctx
    length = codes.shape[1]
    rows = length // 2
    taps, _, width = stem_weight.shape
    half = width // 2
    unit = half // 4
    total = rows * n_ctx
    lanes = -(-(rows + 256) // 128) * 128
    cot = cotangent[0]
    z_bit, y_bit = 2, n_ctx
    x_bit = 4 if n_ctx % 8 == 0 else 2

    def swap(value, even_bit, odd_bit=None):
        odd_bit = even_bit if odd_bit is None else odd_bit
        pairs = [(i, i ^ (odd_bit if i & 1 else even_bit)) for i in range(devices)]
        return lax.ppermute(value, AXES, pairs)

    def call(kernel, out, operands, scratch=(), keep=(), **options):
        if keep:
            options["input_output_aliases"] = {
                len(operands) + k: len(out) + k for k in range(len(keep))
            }
            kernel = holding(kernel, len(operands), len(out), len(keep))
            operands = list(operands) + near_by(*keep)
            out = list(out) + [(value.shape, value.dtype) for value in keep]
        shapes = [jax.ShapeDtypeStruct(o[0], o[1]) for o in out]
        specs = [o[2] if len(o) > 2 else VMEM for o in out]
        options.setdefault("compiler_params", params())
        return pl.pallas_call(
            kernel,
            out_shape=shapes,
            in_specs=[spec for _, spec in operands],
            out_specs=specs,
            scratch_shapes=list(scratch),
            **options,
        )(*[value for value, _ in operands])

    def near_by(*values):
        return [(value, VMEM) for value in values]

    def far_off(*values):
        return [(pltpu.with_memory_space_constraint(value, pltpu.HBM), FAR) for value in values]

    outward = {}
    for d in range(n_dp):
        for c in range(n_ctx):
            other = c + 1 if c & 1 else c - 1
            if 0 <= other < n_ctx:
                outward[d * n_ctx + c] = d * n_ctx + other

    pair_cot = swap(cot, y_bit)
    dma = pltpu.SemaphoreType.DMA
    edge = ((16, lanes), bf16)
    own, near, far = call(
        functools.partial(first_kernel, rows, lanes),
        [edge, edge, edge],
        far_off(codes, variant_pos, variant_shift, cot),
        [
            pltpu.VMEM((1, length), jnp.int32),
            pltpu.SMEM(variant_pos.shape, jnp.int32),
            pltpu.SMEM(variant_pos.shape, jnp.int32),
            pltpu.VMEM((16, width), bf16),
            pltpu.VMEM((16, width), bf16),
            dma((5,)),
        ],
        compiler_params=params(FIRST_LIMIT),
    )
    weight, half_weight, cot_v, conv_v = call(
        second_kernel,
        [
            ((192, 2 * width), bf16),
            ((192, width), bf16),
            (cot.shape, bf16),
            (conv_weight.shape, bf16),
        ],
        far_off(cot, stem_weight, conv_weight) + near_by(near),
        [pltpu.VMEM(stem_weight.shape, f32), dma((3,))],
    )
    near = swap(near, 1)
    cost = pl.CostEstimate(
        flops=2 * TAPS * rows * width * width, bytes_accessed=4 << 20, transcendentals=0
    )
    padded = rows + 2 * LEAD
    far = lax.ppermute(far, AXES, list(outward.items()))
    pair_codes = swap(own + near + far, y_bit)
    stem_half = pltpu.VMEM((width, rows + 128), f32)
    gates = ((TAPS * half, rows), bf16)
    part, edges = call(
        functools.partial(own_kernel, rows, total),
        [((TAPS * half, width), f32), ((16, width), f32)],
        near_by(own, near, far, half_weight, conv_v, cot_v),
        [stem_half, pltpu.VMEM(*gates)],
    )
    (pair_gates,) = call(
        functools.partial(pair_kernel, rows, total),
        [gates],
        near_by(pair_codes, half_weight),
        [stem_half],
    )
    size = TAPS * half // 2
    (sent,) = call(
        functools.partial(sum_kernel, True),
        [((size, width), bf16)],
        near_by(part, pair_gates, pair_cot),
    )
    got = swap(sent, 1)
    (kept,) = call(
        functools.partial(sum_kernel, False),
        [((size, width), f32)],
        near_by(after(part, sent), pair_gates, pair_cot),
    )
    (back,) = call(
        functools.partial(back_kernel, rows),
        [((rows, width), f32)],
        near_by(conv_v, after(cot_v, sent)),
        [pltpu.VMEM((padded, width), bf16)],
        cost_estimate=cost,
    )
    got, back = lax.optimization_barrier((got, back))
    size //= 2
    sent, kept, back = call(
        split_kernel,
        [((size, width), bf16), ((size, width), f32)],
        near_by(kept, got),
        keep=[back],
    )
    got = swap(sent, x_bit, z_bit)
    d_pooled, stem_part, gated, pooled = call(
        functools.partial(slope_kernel, rows, total),
        [
            ((rows, width), bf16),
            ((4 * taps + 4, width), f32),
            ((padded, width), bf16),
            ((rows, width), bf16),
        ],
        near_by(after(own, sent), near, far, weight, back, edges, cot_v),
        [pltpu.VMEM((padded, 2 * width), f32)],
        cost_estimate=cost,
    )
    value = kept + got.astype(f32)

    cut = FIRST * unit
    rest = size - cut
    left = value[:cut]
    right = jnp.concatenate([value[cut:], stem_part], axis=0)
    bits = [1 << k for k in range(devices.bit_length() - 1)]
    even_rest = [b for b in bits if b not in (1, x_bit, y_bit)]
    odd_rest = [b for b in bits if b not in (1, z_bit, y_bit)]
    odd_rest = odd_rest[1:] + odd_rest[:1]
    for k, (b, odd_b) in enumerate(zip(even_rest, odd_rest)):
        left, right = rounded(left), rounded(right)
        if k == 0:
            pooled = after(pooled, right.astype(bf16))
        left, right = [v + swap(v.astype(bf16), b, odd_b).astype(f32) for v in (left, right)]
    (features,) = call(
        functools.partial(feature_kernel, rows),
        [((rows, width), bf16)],
        near_by(gated, pooled, conv_v),
        cost_estimate=cost,
    )
    left, features = together(left, features)
    left = left.astype(bf16)
    stem_sum = right[rest:]
    right = right[:rest].astype(bf16)

    whole = ((TAPS, width, width), f32, FAR)

    def joined(pieces):
        return jnp.concatenate([pieces, stem_sum.astype(bf16)], axis=0)

    stem_sum = rounded(stem_sum)
    got_left, got_right = swap(left, x_bit, y_bit), swap(joined(right), x_bit, y_bit)
    left = jnp.concatenate([left, got_left], axis=0)
    stem_sum = stem_sum + got_right[rest:].astype(f32)
    right = jnp.concatenate([right, got_right[:rest]], axis=0)

    stem_sum = rounded(stem_sum)
    got_left, got_right = swap(left, y_bit, z_bit), swap(joined(right), y_bit, z_bit)
    (conv_grad,) = call(
        early_kernel,
        [whole],
        near_by(left, right, swap(left, 1), swap(right, 1)),
        [pltpu.VMEM((TAPS * 4, unit, width), f32), dma((8,))],
    )
    stem_sum = stem_sum + got_right[2 * rest :].astype(f32)
    left, right = got_left, got_right[: 2 * rest]
    left, conv_grad = together(left, conv_grad)
    got_left, got_right = swap(left, 1), swap(joined(right), 1)
    (conv_grad,) = call(
        late_kernel,
        [whole],
        near_by(left, right, got_left) + far_off(conv_grad),
        [pltpu.VMEM((2 * (TAPS + FIRST), unit, width), f32), dma((6,))],
        input_output_aliases={3: 0},
    )
    conv_grad, stem_grad = call(
        last_kernel,
        [whole, (stem_weight.shape, f32, FAR)],
        near_by(got_right, stem_sum) + far_off(conv_grad),
        [
            pltpu.VMEM((2 * (TAPS - FIRST), unit, width), f32),
            dma((2,)),
            pltpu.VMEM(stem_weight.shape, f32),
            dma,
        ],
        input_output_aliases={2: 0},
    )
    return (features[None], d_pooled[None], conv_grad, stem_grad)


def solution(mesh):
    placed = (P("dp", "context"), P("dp", None), P("dp", None), P(), P(), P("dp", "context", None))
    return jax.shard_map(
        per_device,
        mesh=mesh,
        in_specs=placed,
        out_specs=(P("dp", "context", None), P("dp", "context", None), P(), P()),
        check_vma=False,
    )
```
